256 devices in a mesh: dp: 16 (over x, y_hi, core), seq: 16 (over z, y_lo).
Axes of the slice: x: 4, y: 4 (y_hi: 2, y_lo: 2; y = y_hi * 2 + y_lo), z: 8, core: 2. Of those that a mesh axis runs over, the one named last changes fastest.
Arguments:
- normed_input: bfloat16 [32768, 4096], P(('dp', 'seq')), may hold values from -6 to 6
- queries: bfloat16 [32768, 2048], P(('dp', 'seq')), may hold values from -22 to 22
- rotated_key_rows: bfloat16 [32768, 2048], P(('dp', 'seq')), may hold values from -22 to 22
- frozen_value_rows: bfloat16 [32768, 2048], P(('dp', 'seq')), may hold values from -6 to 6
- cotangent: bfloat16 [32768, 2048], P(('dp', 'seq')), may hold values from -24 to 24
- adapter_down_weight: bfloat16 [4096, 128], replicated, may hold values from -0.09375 to 0.09375
- adapter_up_weight: bfloat16 [128, 2048], replicated, may hold values from -0.5 to 0.5
- document_lengths: int32 [16, 16], P('dp'), may hold values from 1 to 256, 2048 in all within a row
- versions: int32 [16, 16], P('dp'), may hold values from 0 to 3
Outputs:
- query_gradient: bfloat16 [32768, 2048], P(('dp', 'seq'))
- key_gradient: bfloat16 [32768, 2048], P(('dp', 'seq'))
- value_gradient: bfloat16 [32768, 2048], P(('dp', 'seq'))
- down_weight_gradient: float32 [4096, 128], P('dp')
- up_weight_gradient: float32 [128, 2048], P(None, 'dp')
The draws below stay inside these ranges and needn't reach their ends.
Inputs may be any that keep to these rules, and one draw needn't show every extreme that they name: `document_lengths`: each row sums to 2048, and every row has a document of exactly 256 tokens.
All inputs are finite; a program needn't handle non-finite values.
Results may differ from the reference program's by a relative error of at most 0.02.
Values may be sent and summed in bfloat16 or wider, within the bound.
No kernel may reach another device: no remote copies, remote signals or barrier semaphores. Data moves between devices by JAX's collectives and lax.ppermute only.
A program may use at most 128 MiB of HBM per device.

```python
import math
import jax
import jax.numpy as jnp
import numpy as np
from jax import lax

MODEL_WIDTH = 4096
HEADS = 16
HEAD_DIM = 128
ADAPTER_RANK = 128
NDOC = 16
VERSIONS = 4
TOK_DEV = 128
TOK_GROUP = 2048
MOST = 256
GROUPS = 16
TOKEN_TOTAL = 32768
FEATURE_WIDTH = 2048
N_DP = 16
N_SEQ = 16


def draw_queries(key, part):
    key = jax.random.fold_in(key, 11)
    fresh = jnp.clip(jax.random.normal(key, (TOKEN_TOTAL, HEADS * HEAD_DIM), jnp.float32), -4.0, 4.0)
    return fresh.astype(jnp.bfloat16)


def draw_rotated_key_rows(key, part):
    key = jax.random.fold_in(key, 23)
    fresh = jnp.clip(jax.random.normal(key, (TOKEN_TOTAL, HEADS * HEAD_DIM), jnp.float32), -4.0, 4.0)
    return fresh.astype(jnp.bfloat16)


def plant(result, own_key, low, top_value):
    index_at = [jax.random.randint(jax.random.fold_in(own_key, axis), (), 0, length) for axis, length in enumerate(result.shape)]
    longest = result.shape.index(max(result.shape))
    beside = index_at[:longest] + [(index_at[longest] + 1) % result.shape[longest]] + index_at[longest + 1:]
    return result.at[tuple(index_at)].set(low).at[tuple(beside)].set(top_value)


def block_levels(key, shape, shards, smallest, top_value):
    loudness, own = 1.0, jax.random.fold_in(key, 6)
    for position, blocks in shards:
        heights = jnp.exp(jax.random.uniform(jax.random.fold_in(own, position), (blocks,), jnp.float32, smallest / len(shards), top_value / len(shards)))
        loudness = loudness * jnp.repeat(heights, shape[position] // blocks).reshape([-1 if axis == position else 1 for axis in range(len(shape))])
    return loudness


def length_profile(amount, total, reach, slope):
    loads = [(1 << 20) // math.isqrt(grade ** slope) + 1 for grade in range(2, amount + 1)]
    surplus, counts = total - reach - (amount - 1), [1] * (amount - 1)
    while surplus > 0:
        free = [i for i in range(amount - 1) if counts[i] < reach]
        pool, budget = sum([loads[i] for i in free]), surplus
        for i in free:
            extra = min(reach - counts[i], max(1, budget * loads[i] // pool), surplus)
            counts[i] = counts[i] + extra
            surplus = surplus - extra
    return np.array([reach] + counts)


def uneven_parts(rng, number_of, total, limit, skew):
    if number_of == 2:
        one = jax.random.randint(rng, (), max(1, total - limit), min(limit, total - 1) + 1)
        return jnp.stack([one, total - one])
    tallies = jnp.asarray(length_profile(number_of, total, limit, skew), jnp.int32)
    twos = (number_of - 1) // 2
    giver, taker = tallies[1:1 + 2 * twos:2], tallies[2:2 + 2 * twos:2]
    slack = jnp.minimum(giver - 1, limit - taker)
    passed = jax.random.randint(jax.random.fold_in(rng, 1), (twos,), 0, 1 << 20) % (slack + 1)
    tallies = tallies.at[1:1 + 2 * twos:2].set(giver - passed).at[2:2 + 2 * twos:2].set(taker + passed)
    return tallies[jax.random.permutation(jax.random.fold_in(rng, 2), number_of)]


def gaussian(rng, shape, scale, bound, split=(), kind=jnp.bfloat16):
    array = jax.random.normal(rng, shape, jnp.float32) * scale
    if len(split) > 0:
        array = block_levels(rng, shape, split, -0.22, 0.18) * array
    return jnp.clip(array, min=-bound, max=bound).astype(kind)


def setup_inputs(seed: int = 0) -> dict:
    key_of = jax.random.split(jax.random.key(seed), 10)
    normed_input = gaussian(key_of[0], (TOKEN_TOTAL, MODEL_WIDTH), 1.0, 6.0, ((0, 256),))
    queries = draw_queries(jax.random.fold_in(key_of[9], 71), 0)
    rotated_key_rows = draw_rotated_key_rows(jax.random.fold_in(key_of[9], 71), 0)
    frozen_value_rows = gaussian(key_of[3], (TOKEN_TOTAL, FEATURE_WIDTH), 1.0, 6.0, ((0, 256),))
    cotangent = gaussian(key_of[4], (TOKEN_TOTAL, FEATURE_WIDTH), 4.0, 24.0, ((0, 256),))
    adapter_down_weight = gaussian(key_of[5], (MODEL_WIDTH, ADAPTER_RANK), MODEL_WIDTH ** -0.5, 0.09375)
    adapter_up_weight = gaussian(key_of[6], (ADAPTER_RANK, FEATURE_WIDTH), ADAPTER_RANK ** -0.5, 0.5)
    document_lengths = jax.vmap(lambda own: uneven_parts(own, NDOC, TOK_GROUP, MOST, 2))(jax.random.split(key_of[7], GROUPS)).reshape((GROUPS, NDOC)).astype(jnp.int32)
    versions = plant(jax.random.randint(key_of[8], (GROUPS, NDOC), 0, VERSIONS), jax.random.fold_in(key_of[8], 1), 0, VERSIONS - 1).astype(jnp.int32)
    return {"normed_input": normed_input, "queries": queries, "rotated_key_rows": rotated_key_rows, "frozen_value_rows": frozen_value_rows, "cotangent": cotangent, "adapter_down_weight": adapter_down_weight, "adapter_up_weight": adapter_up_weight, "document_lengths": document_lengths, "versions": versions}


adapter_scale = 0.5
masked_score = -1e+30

def document_ids(lengths, positions):
    doc_ends = jnp.cumsum(lengths).astype(jnp.int32)
    inside = (positions >= 0) & (positions < doc_ends[-1])
    doc_index = lax.optimization_barrier(jnp.sum((positions[:, None] >= doc_ends[None, :]).astype(jnp.int32), axis=1)).astype(jnp.int32)
    return jnp.where(inside, doc_index, -1).astype(jnp.int32)

def token_weights(doc_index, doc_versions):
    doc_weight = jnp.exp2((doc_versions - (VERSIONS - 1)).astype(jnp.float32))
    choose = doc_index[:, None] == jnp.arange(doc_versions.shape[0], dtype=jnp.int32)[None, :]
    return lax.optimization_barrier(jnp.sum(jnp.where(choose, doc_weight[None, :], jnp.float32(0.0)), axis=1))

def attend(query_block, key_window, value_window, grad_block, query_doc, key_doc):
    total_row_count = query_block.shape[0]
    width = query_block.shape[1]
    head_count = width // HEAD_DIM
    score_scale = 1.0 / math.sqrt(HEAD_DIM)
    query_heads = query_block.astype(jnp.float32).reshape(total_row_count, head_count, HEAD_DIM)
    key_heads = key_window.astype(jnp.float32).reshape(-1, head_count, HEAD_DIM)
    value_heads = value_window.astype(jnp.float32).reshape(-1, head_count, HEAD_DIM)
    grad_heads = grad_block.astype(jnp.float32).reshape(total_row_count, head_count, HEAD_DIM)
    scores = jnp.einsum('qhd,khd->hqk', query_heads, key_heads) * score_scale
    same_doc = (query_doc[:, None] == key_doc[None, :])[None]
    scores = jnp.where(same_doc, scores, masked_score)
    row_max = lax.optimization_barrier(jnp.max(scores, axis=-1, keepdims=True))
    exponent = jnp.exp(scores - row_max)
    prob = (exponent / lax.optimization_barrier(jnp.sum(exponent, axis=-1, keepdims=True))).astype(jnp.bfloat16)
    prob_full = prob.astype(jnp.float32)
    attended = jnp.einsum('hqk,khd->qhd', prob_full, value_heads)
    dprob = jnp.einsum('qhd,khd->hqk', grad_heads, value_heads)
    row_delta = jnp.einsum('qhd,qhd->hq', grad_heads, attended)
    dscore = (prob_full * (dprob - row_delta[:, :, None]) * score_scale).astype(jnp.bfloat16)
    dscore_full = dscore.astype(jnp.float32)
    gradient_row_block = jnp.einsum('hqk,khd->qhd', dscore_full, key_heads).reshape(total_row_count, width)
    grad_keys = jnp.einsum('hqk,qhd->khd', dscore_full, query_heads).reshape(-1, width)
    grad_values = jnp.einsum('hqk,qhd->khd', prob_full, grad_heads).reshape(-1, width)
    return (gradient_row_block, grad_keys.astype(jnp.bfloat16), grad_values.astype(jnp.bfloat16))

def reference(normed_input, queries, rotated_key_rows, frozen_value_rows, cotangent, adapter_down_weight, adapter_up_weight, document_lengths, versions):
    width = queries.shape[1]
    adapter_value = jnp.dot(normed_input, adapter_down_weight, preferred_element_type=jnp.float32).astype(jnp.bfloat16)
    adapted_values = (frozen_value_rows.astype(jnp.float32) + adapter_scale * jnp.dot(adapter_value, adapter_up_weight, preferred_element_type=jnp.float32)).astype(jnp.bfloat16)
    window_reach = max(1, N_SEQ // 8)
    padding = window_reach * TOK_DEV
    window_rows = (2 * window_reach + 1) * TOK_DEV

    def one_group(group_index):
        start = (group_index * TOK_GROUP).astype(jnp.int32)
        query_slab = lax.dynamic_slice_in_dim(queries, start, TOK_GROUP, 0)
        key_slab = lax.dynamic_slice_in_dim(rotated_key_rows, start, TOK_GROUP, 0)
        value_slab = lax.dynamic_slice_in_dim(adapted_values, start, TOK_GROUP, 0)
        grad_slab = lax.dynamic_slice_in_dim(cotangent, start, TOK_GROUP, 0)
        lengths = lax.dynamic_index_in_dim(document_lengths, group_index, 0, False)
        doc_versions = lax.dynamic_index_in_dim(versions, group_index, 0, False)
        doc_index = document_ids(lengths, jnp.arange(TOK_GROUP, dtype=jnp.int32))
        weights = token_weights(doc_index, doc_versions)
        scaled = (weights[:, None] * grad_slab.astype(jnp.float32)).astype(jnp.bfloat16)
        key_padded = jnp.pad(key_slab, ((padding, padding), (0, 0)))
        value_padded = jnp.pad(value_slab, ((padding, padding), (0, 0)))
        doc_padded = document_ids(lengths, jnp.arange(TOK_GROUP + 2 * padding, dtype=jnp.int32) - padding)

        def per_shard(totals, shard_index):
            first = (shard_index * TOK_DEV).astype(jnp.int32)
            query_block = lax.dynamic_slice_in_dim(query_slab, first, TOK_DEV, 0)
            grad_block = lax.dynamic_slice_in_dim(scaled, first, TOK_DEV, 0)
            query_doc = lax.dynamic_slice_in_dim(doc_index, first, TOK_DEV, 0)
            key_window = lax.dynamic_slice_in_dim(key_padded, first, window_rows, 0)
            value_window = lax.dynamic_slice_in_dim(value_padded, first, window_rows, 0)
            key_doc = lax.dynamic_slice_in_dim(doc_padded, first, window_rows, 0)
            gradient_row_block, grad_keys, grad_values = attend(query_block, key_window, value_window, grad_block, query_doc, key_doc)
            key_total, value_total = totals
            key_part = lax.dynamic_slice_in_dim(key_total, first, window_rows, 0) + grad_keys.astype(jnp.float32)
            value_part = lax.dynamic_slice_in_dim(value_total, first, window_rows, 0) + grad_values.astype(jnp.float32)
            key_total = lax.dynamic_update_slice_in_dim(key_total, key_part, first, 0)
            value_total = lax.dynamic_update_slice_in_dim(value_total, value_part, first, 0)
            return ((key_total, value_total), gradient_row_block.astype(jnp.bfloat16))
        empty = jnp.zeros((TOK_GROUP + 2 * padding, width), jnp.float32)
        totals, gradient_row_block = lax.scan(per_shard, (empty, empty), jnp.arange(N_SEQ, dtype=jnp.int32))
        key_total, value_total = totals
        return (gradient_row_block.reshape(TOK_GROUP, width), key_total[padding:padding + TOK_GROUP].astype(jnp.bfloat16), value_total[padding:padding + TOK_GROUP].astype(jnp.bfloat16))
    query_gradient, key_gradient, value_gradient = lax.map(one_group, jnp.arange(N_DP, dtype=jnp.int32))
    query_gradient = query_gradient.reshape(TOKEN_TOTAL, width)
    key_gradient = key_gradient.reshape(TOKEN_TOTAL, width)
    value_gradient = value_gradient.reshape(TOKEN_TOTAL, width)
    gradient_norm_value = adapter_scale * (1.0 / math.sqrt(TOKEN_TOTAL))
    returned_rows = jnp.dot(value_gradient, adapter_up_weight.T, preferred_element_type=jnp.float32).astype(jnp.bfloat16)
    down_weight_gradient = jnp.dot(normed_input.T, returned_rows, preferred_element_type=jnp.float32) * gradient_norm_value
    up_weight_gradient = jnp.dot(adapter_value.T, value_gradient, preferred_element_type=jnp.float32) * gradient_norm_value
    return (query_gradient, key_gradient, value_gradient, down_weight_gradient, up_weight_gradient)
```

```python
import functools
import math

import jax
import jax.numpy as jnp
from jax import lax
from jax.experimental import pallas as pl
from jax.experimental.pallas import tpu as pltpu
from jax.sharding import PartitionSpec as P

HEAD_DIM = 128
VERSIONS = 4

adapter_scale = 0.5
masked_score = -1e30
VMEM_LIMIT = 48 * 1024 * 1024
HEADS_PER_STEP = 2


def contract(a, b, dim_a, dim_b):
    return lax.dot_general(
        a, b, (((dim_a,), (dim_b,)), ((), ())), preferred_element_type=jnp.float32
    )


def shifted(block, axis, target):
    count = lax.axis_size(axis)
    route = [(i, target(i)) for i in range(count) if 0 <= target(i) < count]
    return lax.ppermute(block, axis, route)


def prepare_kernel(place, x, down, up, frozen, keys, queries, grads, pair_out, ring_out, query_out, value_own, low_out, x_out):
    half = keys.shape[1] // 2
    y = place[0]
    own = pl.multiple_of(y * half, half)
    other = pl.multiple_of((1 - y) * half, half)
    low = contract(x[...], down[...], 1, 0).astype(jnp.bfloat16)
    low_out[...] = low
    pair_out[:, :half] = keys[:, pl.ds(other, half)]
    ring_out[:, :half] = keys[:, pl.ds(own, half)]
    query_out[:, :half] = queries[:, pl.ds(other, half)]
    query_out[:, half:] = grads[:, pl.ds(other, half)]
    share = x.shape[1] // x_out.shape[0]
    for i in range(x_out.shape[0]):
        x_out[i] = x[:, i * share : (i + 1) * share]

    def values(start):
        lifted = contract(low, up[:, pl.ds(start, half)], 1, 0)
        base = frozen[:, pl.ds(start, half)].astype(jnp.float32)
        return (base + adapter_scale * lifted).astype(jnp.bfloat16)

    pair_out[:, half : 2 * half] = values(other)
    pair_out[:, 2 * half :] = low
    mine = values(own)
    ring_out[:, half:] = mine
    value_own[...] = mine


def prepare(place, x, down, up, frozen, keys, queries, grads, replicas):
    rows, width = keys.shape
    rank = down.shape[1]
    half = width // 2
    kind = jnp.bfloat16
    shapes = [
        (rows, width + rank),
        (rows, width),
        (rows, width),
        (rows, half),
        (rows, rank),
        (replicas, rows, x.shape[1] // replicas),
    ]
    vmem = pl.BlockSpec(memory_space=pltpu.VMEM)
    return pl.pallas_call(
        prepare_kernel,
        out_shape=[jax.ShapeDtypeStruct(s, kind) for s in shapes],
        in_specs=[pl.BlockSpec(memory_space=pltpu.SMEM)] + [vmem] * 7,
        out_specs=[vmem] * 6,
        compiler_params=pltpu.CompilerParams(vmem_limit_bytes=VMEM_LIMIT),
    )(place, x, down, up, frozen, keys, queries, grads)


def attend_kernel(
    place, lengths, versions,
    q_own, q_pair, g_own, g_pair,
    k_own, k_pair, k_prev, k_prev2, k_next, k_next2,
    v_own, v_pair, v_prev, v_prev2, v_next, v_next2,
    l_own, l_pair, l_prev, l_prev2, l_next, l_next2,
    up,
    dq_own, dq_pair, mid, prev, nxt, back, up_part,
    bias, weight, low,
):
    rows = q_own.shape[0]
    documents = lengths.shape[1]
    step = pl.program_id(0)
    y, z = place[0], place[1]
    own_base = (2 * z + y) * rows
    pair_base = (2 * z + 1 - y) * rows
    bases = [own_base, pair_base]
    for shift in (-2 * rows, 2 * rows):
        bases += [own_base + shift, pair_base + shift]

    @pl.when(step == 0)
    def _():
        ends, total = [], jnp.int32(0)
        for j in range(documents):
            total = total + lengths[0, j]
            ends.append(total)
        for b in range(2):
            pos = lax.broadcasted_iota(jnp.int32, (8, rows), 1) + bases[b]
            first = jnp.zeros_like(pos)
            last = jnp.zeros_like(pos)
            for j in range(documents):
                first = jnp.where(pos >= ends[j], ends[j], first)
            for j in reversed(range(documents)):
                last = jnp.where(pos < ends[j], ends[j], last)
            first, last = first[:1], last[:1]
            for c in range(6):
                key_pos = lax.broadcasted_iota(jnp.int32, (rows, rows), 0) + bases[c]
                inside = (key_pos >= first) & (key_pos < last)
                bias[c * rows : (c + 1) * rows, b * rows : (b + 1) * rows] = jnp.where(
                    inside, jnp.float32(0.0), jnp.float32(masked_score)
                )
            row_pos = lax.broadcasted_iota(jnp.int32, (rows, HEAD_DIM), 0) + bases[b]
            scale = jnp.zeros((rows, HEAD_DIM), jnp.float32)
            for j in range(documents):
                level = lax.shift_left(jnp.int32(1), versions[0, j]).astype(jnp.float32)
                level = level * (2.0 ** (1 - VERSIONS))
                begin = ends[j - 1] if j > 0 else 0
                scale = jnp.where(row_pos >= begin, level, scale)
            weight[b * rows : (b + 1) * rows, :] = scale
        for c, ref in enumerate((l_own, l_pair, l_prev, l_prev2, l_next, l_next2)):
            low[c * rows : (c + 1) * rows, :] = ref[...]
        back[...] = jnp.zeros_like(back)

    score_scale = 1.0 / math.sqrt(HEAD_DIM)
    log2e = 1.4426950408889634
    for h in range(HEADS_PER_STEP):
        cols = slice(h * HEAD_DIM, (h + 1) * HEAD_DIM)
        gather = lambda *refs: jnp.concatenate([r[:, cols] for r in refs], axis=0)
        q = gather(q_own, q_pair)
        k = gather(k_own, k_pair, k_prev, k_prev2, k_next, k_next2)
        v = gather(v_own, v_pair, v_prev, v_prev2, v_next, v_next2)
        g = (weight[...] * gather(g_own, g_pair).astype(jnp.float32)).astype(jnp.bfloat16)
        s = contract(k, q, 1, 1) * (score_scale * log2e) + bias[...]
        e = jnp.exp2(s - jnp.max(s, axis=0, keepdims=True))
        p = (e * (1.0 / jnp.sum(e, axis=0, keepdims=True))).astype(jnp.bfloat16)
        dv = contract(p, g, 1, 0)
        mid[1, :, cols] = dv[: 2 * rows]
        dv_small = dv.astype(jnp.bfloat16)
        prev[1, :, cols] = dv_small[2 * rows : 4 * rows]
        nxt[1, :, cols] = dv_small[4 * rows :]
        back[...] += contract(dv_small, up[:, cols], 1, 1)
        up_part[h] = contract(low[...], dv_small, 0, 0)
        dp = contract(v, g, 1, 1)
        wide = p.astype(jnp.float32)
        delta = jnp.sum(wide * dp, axis=0, keepdims=True)
        ds = (wide * (dp - delta) * score_scale).astype(jnp.bfloat16)
        dk = contract(ds, q, 1, 0)
        mid[0, :, cols] = dk[: 2 * rows]
        prev[0, :, cols] = dk[2 * rows : 4 * rows].astype(jnp.bfloat16)
        nxt[0, :, cols] = dk[4 * rows :].astype(jnp.bfloat16)
        dq = contract(ds, k, 0, 0).astype(jnp.bfloat16)
        dq_own[:, cols] = dq[:rows]
        dq_pair[:, cols] = dq[rows:]


def attend(place, lengths, versions, queries, grads, keys, value_own, low, up, pair, pair_q, prev, prev2, nxt, nxt2):
    rows, width = queries.shape
    rank = low.shape[1]
    half = width // 2
    heads = half // HEAD_DIM
    block = HEADS_PER_STEP * HEAD_DIM
    steps = heads // HEADS_PER_STEP
    whole = lambda h, pc, *_: (0, pc[0] * steps + h)
    at = lambda first: pl.BlockSpec((rows, block), lambda h, *_: (0, first + h))
    mine = pl.BlockSpec((rows, block), whole)
    low_at = lambda b: pl.BlockSpec((rows, rank), lambda h, *_: (0, b))
    tail = width // rank
    kind = jnp.bfloat16
    in_specs = [
        mine, at(0), mine, at(steps),
        mine, at(0), at(0), at(0), at(0), at(0),
        at(0), at(steps), at(steps), at(steps), at(steps), at(steps),
        low_at(0), low_at(tail), low_at(tail), low_at(tail + 1), low_at(tail), low_at(tail + 1),
        pl.BlockSpec((rank, block), whole),
    ]
    operands = (
        queries, pair_q, grads, pair_q,
        keys, pair, prev, prev2, nxt, nxt2,
        value_own, pair, prev, prev2, nxt, nxt2,
        low, pair, prev2, prev2, nxt2, nxt2,
        up,
    )
    out_shape = [
        jax.ShapeDtypeStruct((rows, half), kind),
        jax.ShapeDtypeStruct((rows, half), kind),
        jax.ShapeDtypeStruct((2, 2 * rows, half), jnp.float32),
        jax.ShapeDtypeStruct((2, 2 * rows, half), kind),
        jax.ShapeDtypeStruct((2, 2 * rows, half), kind),
        jax.ShapeDtypeStruct((6 * rows, rank), jnp.float32),
        jax.ShapeDtypeStruct((heads, rank, HEAD_DIM), jnp.float32),
    ]
    triple = pl.BlockSpec((2, 2 * rows, block), lambda h, *_: (0, 0, h))
    out_specs = [
        at(0), at(0), triple, triple, triple,
        pl.BlockSpec((6 * rows, rank), lambda h, *_: (0, 0)),
        pl.BlockSpec((HEADS_PER_STEP, rank, HEAD_DIM), lambda h, *_: (h, 0, 0)),
    ]
    pairs = 12 * rows * rows * heads
    return pl.pallas_call(
        attend_kernel,
        grid_spec=pltpu.PrefetchScalarGridSpec(
            num_scalar_prefetch=3,
            grid=(steps,),
            in_specs=in_specs,
            out_specs=out_specs,
            scratch_shapes=[
                pltpu.VMEM((6 * rows, 2 * rows), jnp.float32),
                pltpu.VMEM((2 * rows, HEAD_DIM), jnp.float32),
                pltpu.VMEM((6 * rows, rank), kind),
            ],
        ),
        out_shape=out_shape,
        compiler_params=pltpu.CompilerParams(
            vmem_limit_bytes=VMEM_LIMIT, dimension_semantics=("arbitrary",)
        ),
        cost_estimate=pl.CostEstimate(
            flops=10 * pairs * HEAD_DIM, bytes_accessed=12 << 20, transcendentals=pairs
        ),
    )(place, lengths, versions, *operands)


def per_device(
    normed_input, queries, rotated_key_rows, frozen_value_rows, cotangent,
    adapter_down_weight, adapter_up_weight, document_lengths, versions,
):
    rows, width = queries.shape
    half = width // 2
    rank = adapter_down_weight.shape[1]
    sequence_count = lax.axis_size("seq")
    replicas = lax.axis_size("dp")
    shard = lax.axis_index("seq")
    replica = lax.axis_index("dp")
    y, z = shard % 2, shard // 2
    place = jnp.stack([y, z]).astype(jnp.int32)

    pair_send, ring_send, query_send, value_own, low, x_send = prepare(
        place, normed_input, adapter_down_weight, adapter_up_weight, frozen_value_rows,
        rotated_key_rows, queries, cotangent, replicas,
    )
    to_pair = lambda a: shifted(a, "seq", lambda i: i ^ 1)
    to_next = lambda a: shifted(a, "seq", lambda i: i + 2)
    to_prev = lambda a: shifted(a, "seq", lambda i: i - 2)
    pair = to_pair(pair_send)
    prev, nxt = to_next(ring_send), to_prev(ring_send)
    pair_q = to_pair(query_send)
    second = jnp.concatenate([pair[:, :width], low, pair[:, width:]], axis=1)
    prev2, nxt2 = to_next(second), to_prev(second)

    dq_own, dq_pair, mid, out_prev, out_next, back, up_part = attend(
        place, document_lengths, versions, queries, cotangent, rotated_key_rows, value_own, low,
        adapter_up_weight, pair, pair_q, prev, prev2, nxt, nxt2,
    )
    x_cols = lax.all_to_all(x_send, "dp", 0, 0, tiled=True)

    blocks = [back[i * rows : (i + 1) * rows] for i in range(6)]
    arrived = blocks[0] + to_pair(blocks[1])
    arrived = arrived + to_prev(blocks[2]) + to_next(blocks[4])
    arrived = arrived + shifted(blocks[3], "seq", lambda i: i - 1 if i % 2 == 0 else i - 3)
    arrived = arrived + shifted(blocks[5], "seq", lambda i: i + 3 if i % 2 == 0 else i + 1)
    returned_rows = arrived.astype(jnp.bfloat16)
    spread = jnp.broadcast_to(returned_rows[None], (replicas,) + returned_rows.shape)
    rows_all = lax.all_to_all(spread, "dp", 0, 0, tiled=True)

    empty = jnp.zeros_like(up_part)
    up_send = jnp.where(
        y == 0,
        jnp.concatenate([up_part, empty], axis=0),
        jnp.concatenate([empty, up_part], axis=0),
    ).astype(jnp.bfloat16)
    up_all = lax.all_to_all(up_send, "dp", 0, 0, tiled=True)
    up_mine = jnp.sum(up_all.astype(jnp.float32), axis=0)
    norm = adapter_scale / math.sqrt(rows * sequence_count * replicas)
    down_mine = lax.dot_general(
        x_cols, rows_all, (((0, 1), (0, 1)), ((), ())), preferred_element_type=jnp.float32
    )
    joined = jnp.concatenate([down_mine, up_mine], axis=0) * norm
    share = joined.shape[0] // sequence_count
    parts = lax.all_to_all(joined.reshape(sequence_count, share, rank), "seq", 0, 0, tiled=True)
    reduced = jnp.sum(parts, axis=0)
    spread = jnp.broadcast_to(reduced[None], (sequence_count, share, rank))
    final = lax.all_to_all(spread, "seq", 0, 0, tiled=True).reshape(sequence_count * share, rank)
    down_rows = adapter_down_weight.shape[0] // replicas
    down_weight_gradient = final[:down_rows]
    up_weight_gradient = final[down_rows:]

    total = mid + to_prev(out_prev).astype(jnp.float32) + to_next(out_next).astype(jnp.float32)
    total = total.astype(jnp.bfloat16)
    send = jnp.concatenate([total[:, rows:], dq_pair[None]], axis=0)
    came = to_pair(send)
    kept = jnp.concatenate([total[:, :rows], dq_own[None]], axis=0)
    whole = jnp.where(
        y == 0, jnp.concatenate([kept, came], axis=2), jnp.concatenate([came, kept], axis=2)
    )
    return (whole[2], whole[0], whole[1], down_weight_gradient, up_weight_gradient)


def solution(mesh):
    tokens = P(("dp", "seq"), None)
    in_specs = (tokens,) * 5 + (P(), P(), P("dp", None), P("dp", None))
    out_specs = (tokens,) * 3 + (P("dp", None), P(None, "dp"))
    return jax.shard_map(
        per_device, mesh=mesh, in_specs=in_specs, out_specs=out_specs, check_vma=False
    )
```

```python
import functools
import math

import jax
import jax.numpy as jnp
from jax import lax
from jax.experimental import pallas as pl
from jax.experimental.pallas import tpu as pltpu
from jax.sharding import PartitionSpec as P

HEAD_DIM = 128
VERSIONS = 4

adapter_scale = 0.5
masked_score = -1e30
VMEM_LIMIT = 60 * 1024 * 1024
HEADS_PER_STEP = 4


def contract(a, b, dim_a, dim_b):
    return lax.dot_general(
        a, b, (((dim_a,), (dim_b,)), ((), ())), preferred_element_type=jnp.float32
    )


def shifted(block, axis, target):
    count = lax.axis_size(axis)
    route = [(i, target(i)) for i in range(count) if 0 <= target(i) < count]
    return lax.ppermute(block, axis, route)


def prepare_kernel(
    place, x, down, up, frozen, keys, queries, grads,
    pair_out, ring_out, query_out,
    x_in, down_in, up_in, frozen_in, moved, values_v, low_v, sems,
):
    rows, rank = low_v.shape
    half = values_v.shape[2]
    y = place[0]
    own = pl.multiple_of(y * half, half)
    other = pl.multiple_of((1 - y) * half, half)
    used = []

    def copy(src, dst):
        done = pltpu.make_async_copy(src, dst, sems.at[len(used)])
        used.append(done)
        done.start()
        return done

    chunks = 4
    size = x.shape[1] // chunks
    parts = []
    for c in range(chunks):
        span = pl.ds(c * size, size)
        parts.append((copy(x.at[:, span], x_in.at[:, span]), copy(down.at[span], down_in.at[span])))
    left, right = pl.ds(0, half), pl.ds(half, half)
    route = [
        (keys, other, pair_out.at[:, left]),
        (keys, own, ring_out.at[:, left]),
        (queries, other, query_out.at[:, left]),
        (grads, other, query_out.at[:, right]),
    ]
    arriving = [copy(src.at[:, pl.ds(at, half)], moved.at[i]) for i, (src, at, _) in enumerate(route)]
    up_done = copy(up, up_in)
    frozen_done = copy(frozen, frozen_in)
    low = jnp.zeros((rows, rank), jnp.float32)
    for c, (a, b) in enumerate(parts):
        a.wait()
        b.wait()
        low += contract(x_in[:, c * size : (c + 1) * size], down_in[c * size : (c + 1) * size, :], 1, 0)
    low = low.astype(jnp.bfloat16)
    low_v[...] = low
    rest = []
    for target in (pair_out.at[:, pl.ds(2 * half, rank)], ring_out.at[:, pl.ds(2 * half, rank)]):
        rest.append(copy(low_v, target))
    for i, done in enumerate(arriving):
        done.wait()
        rest.append(copy(moved.at[i], route[i][2]))
    up_done.wait()
    frozen_done.wait()
    for i, (start, target) in enumerate(((other, pair_out.at[:, right]), (own, ring_out.at[:, right]))):
        lifted = contract(low, up_in[:, pl.ds(start, half)], 1, 0)
        base = frozen_in[:, pl.ds(start, half)].astype(jnp.float32)
        values_v[i] = (base + adapter_scale * lifted).astype(jnp.bfloat16)
        rest.append(copy(values_v.at[i], target))
    for done in rest:
        done.wait()


def prepare(place, x, down, up, frozen, keys, queries, grads):
    rows, width = keys.shape
    rank = down.shape[1]
    half = width // 2
    kind = jnp.bfloat16
    shapes = [(rows, width + rank), (rows, width + rank), (rows, width)]
    anywhere = pl.BlockSpec(memory_space=pl.ANY)
    return pl.pallas_call(
        prepare_kernel,
        out_shape=[jax.ShapeDtypeStruct(s, kind) for s in shapes],
        in_specs=[pl.BlockSpec(memory_space=pltpu.SMEM)] + [anywhere] * 7,
        out_specs=[anywhere] * 3,
        scratch_shapes=[
            pltpu.VMEM(x.shape, kind),
            pltpu.VMEM(down.shape, kind),
            pltpu.VMEM(up.shape, kind),
            pltpu.VMEM(frozen.shape, kind),
            pltpu.VMEM((4, rows, half), kind),
            pltpu.VMEM((2, rows, half), kind),
            pltpu.VMEM((rows, rank), kind),
            pltpu.SemaphoreType.DMA((22,)),
        ],
        compiler_params=pltpu.CompilerParams(vmem_limit_bytes=VMEM_LIMIT),
    )(place, x, down, up, frozen, keys, queries, grads)


def gather(refs, cols):
    return jnp.concatenate([r[:, cols] for r in refs], axis=0)


def against(main, far_a, far_b, other):
    rows = far_a.shape[0]
    far = jnp.concatenate(
        [contract(far_a, other[:rows], 1, 1), contract(far_b, other[rows:], 1, 1)], axis=1
    )
    return jnp.concatenate([contract(main, other, 1, 1), far], axis=0)


def onto(grid, other):
    rows = other.shape[0] // 2
    near = 4 * rows
    return (
        contract(grid[:near], other, 1, 0),
        contract(grid[near:, :rows], other[:rows], 1, 0),
        contract(grid[near:, rows:], other[rows:], 1, 0),
    )


def ordered(order, own, pair, prev, prev2, nxt, nxt2):
    pick = lambda a, b: (a, b) if order == 0 else (b, a)
    mid0, mid1 = pick(own, pair)
    far_prev, near_prev = pick(prev, prev2)
    near_next, far_next = pick(nxt, nxt2)
    return (near_prev, mid0, mid1, near_next), far_prev, far_next


def scatter(order, mid, prev, nxt, cols, main, far_a, far_b):
    rows = far_a.shape[0]
    first, second = (0, rows) if order == 0 else (rows, 0)

    def put(ref, at, val):
        ref[at : at + rows, cols] = val

    put(prev, second, main[:rows])
    put(mid, first, main[rows : 2 * rows])
    put(mid, second, main[2 * rows : 3 * rows])
    put(nxt, first, main[3 * rows :])
    put(prev, first, far_a)
    put(nxt, second, far_b)


def attend_kernel(
    place, lengths, versions,
    q_own, q_pair, g_own, g_pair,
    k_own, k_pair, k_prev, k_prev2, k_next, k_next2,
    v_own, v_pair, v_prev, v_prev2, v_next, v_next2,
    l_own, l_pair, l_prev, l_prev2, l_next, l_next2,
    up,
    dq_own, dq_pair, mid, prev, nxt, back_mid, back_prev, back_next, up_send,
    bias, weight, dvs,
):
    rows = q_own.shape[0]
    documents = lengths.shape[1]
    step = pl.program_id(0)
    y, z = place[0], place[1]
    base = 2 * z * rows
    heads = dvs.shape[1] // HEAD_DIM

    @pl.when(step == 0)
    def _():
        ends, total = [], jnp.int32(0)
        for j in range(documents):
            total = total + lengths[0, j]
            ends.append(total)
        for b in range(2):
            pos = lax.broadcasted_iota(jnp.int32, (8, rows), 1) + base + b * rows
            first = jnp.zeros_like(pos)
            last = jnp.zeros_like(pos)
            for j in range(documents):
                first = jnp.where(pos >= ends[j], ends[j], first)
            for j in reversed(range(documents)):
                last = jnp.where(pos < ends[j], ends[j], last)
            first, last = first[:1], last[:1]
            for c, shift in enumerate((-1, 0, 1, 2, -2 if b == 0 else 3)):
                key_pos = lax.broadcasted_iota(jnp.int32, (rows, rows), 0) + base + shift * rows
                inside = (key_pos >= first) & (key_pos < last)
                bias[c * rows : (c + 1) * rows, b * rows : (b + 1) * rows] = jnp.where(
                    inside, jnp.float32(0.0), jnp.float32(masked_score)
                )
            row_pos = lax.broadcasted_iota(jnp.int32, (rows, HEAD_DIM), 0) + base + b * rows
            scale = jnp.zeros((rows, HEAD_DIM), jnp.float32)
            for j in range(documents):
                level = lax.shift_left(jnp.int32(1), versions[0, j]).astype(jnp.float32)
                level = level * (2.0 ** (1 - VERSIONS))
                begin = ends[j - 1] if j > 0 else 0
                scale = jnp.where(row_pos >= begin, level, scale)
            weight[b * rows : (b + 1) * rows, :] = scale

    score_scale = 1.0 / math.sqrt(HEAD_DIM)
    factor = math.log2(math.e) * score_scale
    near = 4 * rows

    def work(order):
        pick = lambda own, pair: (own, pair) if order == 0 else (pair, own)
        ks, k_fp, k_fn = ordered(order, k_own, k_pair, k_prev, k_prev2, k_next, k_next2)
        vs, v_fp, v_fn = ordered(order, v_own, v_pair, v_prev, v_prev2, v_next, v_next2)
        dq0, dq1 = pick(dq_own, dq_pair)
        for h in range(HEADS_PER_STEP):
            cols = slice(h * HEAD_DIM, (h + 1) * HEAD_DIM)
            q = gather(pick(q_own, q_pair), cols)
            g = weight[...] * gather(pick(g_own, g_pair), cols).astype(jnp.float32)
            g = g.astype(jnp.bfloat16)
            k = gather(ks, cols)
            s = against(k, k_fp[:, cols], k_fn[:, cols], q) * factor + bias[...]
            e = jnp.exp2(s - jnp.max(s, axis=0, keepdims=True))
            wide = e * (1.0 / jnp.sum(e, axis=0, keepdims=True))
            p = wide.astype(jnp.bfloat16)
            small = [a.astype(jnp.bfloat16) for a in onto(p, g)]
            scatter(order, mid.at[1], prev.at[1], nxt.at[1], cols, *small)
            at = step * (HEADS_PER_STEP * HEAD_DIM)
            at = pl.ds(pl.multiple_of(at, HEAD_DIM) + h * HEAD_DIM, HEAD_DIM)
            dvs[:near, at] = small[0]
            dvs[near : near + rows, at] = small[1]
            dvs[near + rows :, at] = small[2]
            dp = against(gather(vs, cols), v_fp[:, cols], v_fn[:, cols], g)
            delta = jnp.sum(wide * dp, axis=0, keepdims=True)
            ds = (wide * (dp - delta)).astype(jnp.bfloat16)
            small = [(score_scale * a).astype(jnp.bfloat16) for a in onto(ds, q)]
            scatter(order, mid.at[0], prev.at[0], nxt.at[0], cols, *small)
            far = jnp.concatenate(
                [
                    contract(ds[near:, :rows], k_fp[:, cols], 0, 0),
                    contract(ds[near:, rows:], k_fn[:, cols], 0, 0),
                ],
                axis=0,
            )
            dq = contract(ds[:near], k, 0, 0) + far
            dq = (dq * score_scale).astype(jnp.bfloat16)
            dq0[:, cols] = dq[:rows]
            dq1[:, cols] = dq[rows:]

        @pl.when(step == pl.num_programs(0) - 1)
        def _():
            ls, l_fp, l_fn = ordered(order, l_own, l_pair, l_prev, l_prev2, l_next, l_next2)
            low = jnp.concatenate([r[...] for r in (*ls, l_fp, l_fn)], axis=0)
            part = contract(low, dvs[...], 0, 0).astype(jnp.bfloat16)
            for h in range(heads):
                up_send[order * heads + h] = part[:, h * HEAD_DIM : (h + 1) * HEAD_DIM]
                up_send[(1 - order) * heads + h] = jnp.zeros((part.shape[0], HEAD_DIM), jnp.bfloat16)
            full = contract(dvs[...], up[...], 1, 1)
            a, b = (0, rows) if order == 0 else (rows, 0)
            places = (
                (back_prev, b), (back_mid, a), (back_mid, b), (back_next, a), (back_prev, a), (back_next, b),
            )
            for c, (ref, at) in enumerate(places):
                ref[at : at + rows, :] = full[c * rows : (c + 1) * rows]

    for order in range(2):
        pl.when(y == order)(functools.partial(work, order))


def attend(place, lengths, versions, queries, grads, keys, ring, up, pair_q, pair, prev, prev2, nxt, nxt2):
    rows, width = queries.shape
    rank = up.shape[0]
    half = width // 2
    heads = half // HEAD_DIM
    block = HEADS_PER_STEP * HEAD_DIM
    steps = heads // HEADS_PER_STEP
    at = lambda first: pl.BlockSpec((rows, block), lambda h, *_: (0, first + h))
    mine = pl.BlockSpec((rows, block), lambda h, pc, *_: (0, pc[0] * steps + h))
    low_at = lambda b: pl.BlockSpec((rows, rank), lambda h, *_: (0, b))
    kind = jnp.bfloat16
    last = half // rank
    in_specs = [
        mine, at(0), mine, at(steps),
        mine, at(0), at(0), at(0), at(0), at(0),
    ] + [at(steps)] * 6 + [low_at(2 * last)] * 6 + [
        pl.BlockSpec((rank, half), lambda h, pc, *_: (0, pc[0])),
    ]
    operands = (
        queries, pair_q, grads, pair_q,
        keys, pair, prev, prev2, nxt, nxt2,
        ring, pair, prev, prev2, nxt, nxt2,
        ring, pair, prev, prev2, nxt, nxt2,
        up,
    )
    single = jax.ShapeDtypeStruct((rows, half), kind)
    double = jax.ShapeDtypeStruct((2, 2 * rows, half), kind)
    back = jax.ShapeDtypeStruct((2 * rows, rank), jnp.float32)
    double_spec = pl.BlockSpec((2, 2 * rows, block), lambda h, *_: (0, 0, h))
    back_spec = pl.BlockSpec((2 * rows, rank), lambda h, *_: (0, 0))
    out_shape = [
        single, single, double, double, double,
        back, back, back,
        jax.ShapeDtypeStruct((2 * heads, rank, HEAD_DIM), kind),
    ]
    out_specs = [
        at(0), at(0), double_spec, double_spec, double_spec,
        back_spec, back_spec, back_spec,
        pl.BlockSpec((2 * heads, rank, HEAD_DIM), lambda h, *_: (0, 0, 0)),
    ]
    pairs = 10 * rows * rows * heads
    return pl.pallas_call(
        attend_kernel,
        grid_spec=pltpu.PrefetchScalarGridSpec(
            num_scalar_prefetch=3,
            grid=(steps,),
            in_specs=in_specs,
            out_specs=out_specs,
            scratch_shapes=[
                pltpu.VMEM((5 * rows, 2 * rows), jnp.float32),
                pltpu.VMEM((2 * rows, HEAD_DIM), jnp.float32),
                pltpu.VMEM((6 * rows, half), kind),
            ],
        ),
        out_shape=out_shape,
        compiler_params=pltpu.CompilerParams(
            vmem_limit_bytes=VMEM_LIMIT, dimension_semantics=("arbitrary",)
        ),
        cost_estimate=pl.CostEstimate(
            flops=10 * pairs * HEAD_DIM, bytes_accessed=12 << 20, transcendentals=pairs
        ),
    )(place, lengths, versions, *operands)


def spread_kernel(mine, from_next, from_prev, theirs, x, up_send, out):
    rows, rank = theirs.shape
    share = out.shape[2] - rank
    back_rows = mine[:rows] + from_next[:rows] + from_prev[:rows] + theirs[...]
    back_rows = back_rows.astype(jnp.bfloat16)
    part = contract(back_rows, x[...], 0, 0).astype(jnp.bfloat16)
    for i in range(out.shape[0]):
        out[i, :, :share] = part[:, i * share : (i + 1) * share]
        out[i, :, share:] = up_send[i]


def spread(mine, from_next, from_prev, theirs, x, up_send):
    rows, rank = theirs.shape
    replicas = up_send.shape[0]
    share = x.shape[1] // replicas
    steps = 1
    each = replicas // steps
    full = lambda a: pl.BlockSpec(a.shape, lambda i: (0, 0))
    return pl.pallas_call(
        spread_kernel,
        grid=(steps,),
        out_shape=jax.ShapeDtypeStruct((replicas, rank, share + HEAD_DIM), jnp.bfloat16),
        in_specs=[
            full(mine), full(from_next), full(from_prev), full(theirs),
            pl.BlockSpec((rows, each * share), lambda i: (0, i)),
            pl.BlockSpec((each, rank, HEAD_DIM), lambda i: (i, 0, 0)),
        ],
        out_specs=pl.BlockSpec((each, rank, share + HEAD_DIM), lambda i: (i, 0, 0)),
        compiler_params=pltpu.CompilerParams(vmem_limit_bytes=VMEM_LIMIT),
    )(mine, from_next, from_prev, theirs, x, up_send)


def fold_kernel(place, parts, keep, send, *, norm):
    rank = parts.shape[1]
    total = parts[0].astype(jnp.float32)
    for i in range(1, parts.shape[0]):
        total = total + parts[i].astype(jnp.float32)
    total = total * norm
    share = total.shape[1] - HEAD_DIM
    down, up = total[:, :share].T, total[:, share:]
    cut = share // 2

    def write(first, second):
        first[:cut] = down[:cut]
        first[cut:] = up[: rank // 2]
        second[:cut] = down[cut:]
        second[cut:] = up[rank // 2 :]

    pl.when(place[0] == 0)(lambda: write(keep, send))
    pl.when(place[0] == 1)(lambda: write(send, keep))


def assemble_kernel(place, both, dq, pair_both, pair_dq, dk_out, dv_out, dq_out):
    rows, half = dq.shape

    def write(own, other):
        dk_out[:, own] = both[0, :rows]
        dv_out[:, own] = both[1, :rows]
        dq_out[:, own] = dq[...]
        dk_out[:, other] = pair_both[0]
        dv_out[:, other] = pair_both[1]
        dq_out[:, other] = pair_dq[...]

    left, right = slice(0, half), slice(half, 2 * half)
    pl.when(place[0] == 0)(lambda: write(left, right))
    pl.when(place[0] == 1)(lambda: write(right, left))


def simple(kernel, out_shape, place, *operands):
    smem, spec = pl.BlockSpec(memory_space=pltpu.SMEM), pl.BlockSpec(memory_space=pltpu.VMEM)
    return pl.pallas_call(
        kernel,
        out_shape=out_shape,
        in_specs=[smem] + [spec] * len(operands),
        out_specs=[spec] * len(out_shape),
        compiler_params=pltpu.CompilerParams(vmem_limit_bytes=VMEM_LIMIT),
    )(place, *operands)


def per_device(
    normed_input, queries, rotated_key_rows, frozen_value_rows, cotangent,
    adapter_down_weight, adapter_up_weight, document_lengths, versions,
):
    rows, width = queries.shape
    half = width // 2
    rank = adapter_down_weight.shape[1]
    sequence_count = lax.axis_size("seq")
    replicas = lax.axis_size("dp")
    shard = lax.axis_index("seq")
    y, z = shard % 2, shard // 2
    place = jnp.stack([y, z]).astype(jnp.int32)
    to_pair = lambda a: shifted(a, "seq", lambda i: i ^ 1)
    to_next = lambda a: shifted(a, "seq", lambda i: i + 2)
    to_prev = lambda a: shifted(a, "seq", lambda i: i - 2)
    after = lambda *a: lax.optimization_barrier(a)
    shape = jax.ShapeDtypeStruct
    wide, narrow = jnp.float32, jnp.bfloat16

    pair_send, ring, q_send = prepare(
        place, normed_input, adapter_down_weight, adapter_up_weight, frozen_value_rows,
        rotated_key_rows, queries, cotangent,
    )
    pair, prev, nxt = to_pair(pair_send), to_next(ring), to_prev(ring)
    pair, q_send = after(pair, q_send)
    prev2, nxt2 = to_next(pair), to_prev(pair)
    q_pair = to_pair(q_send)

    dq, dq_send, mid, out_prev, out_next, back, back_prev, back_next, up_send = attend(
        place, document_lengths, versions, queries, cotangent, rotated_key_rows, ring,
        adapter_up_weight, q_pair, pair, prev, prev2, nxt, nxt2,
    )
    from_next, from_prev = to_prev(back_prev), to_next(back_next)
    from_next, from_prev, dq_send, out_prev, out_next = after(
        from_next, from_prev, dq_send, out_prev, out_next
    )
    theirs = to_pair(back[rows:] + from_next[rows:] + from_prev[rows:])
    payload = spread(back, from_next, from_prev, theirs, normed_input, up_send)
    parts = lax.all_to_all(payload, "dp", 0, 0, tiled=True)
    dq_came = to_pair(dq_send)
    total = mid.astype(wide) + to_prev(out_prev).astype(wide) + to_next(out_next).astype(wide)
    total = total.astype(narrow)

    norm = adapter_scale / math.sqrt(rows * sequence_count * replicas)
    piece = shape(((parts.shape[2] - HEAD_DIM + rank) // 2, rank), wide)
    keep, give = simple(functools.partial(fold_kernel, norm=norm), [piece, piece], place, parts)
    given = to_pair(give)
    given, total_send = after(given, total[:, rows:])
    came = to_pair(total_send)
    count = sequence_count // 2
    columns = [list(range(c, sequence_count, 2)) for c in range(2)]
    copies = jnp.broadcast_to((keep + given).astype(narrow)[None], (count,) + keep.shape)
    sums = lax.all_to_all(copies, "seq", 0, 0, tiled=True, axis_index_groups=columns)
    mine = jnp.sum(sums.astype(wide), axis=0)
    other = to_pair(mine)
    whole = shape((rows, width), narrow)
    dk, dv, dq = simple(assemble_kernel, [whole] * 3, place, total, dq, came, dq_came)
    halves = [jnp.where(y == 0, mine, other), jnp.where(y == 0, other, mine)]
    cut = mine.shape[0] - rank // 2
    down_gradient = jnp.concatenate([a[:cut] for a in halves], axis=0)
    up_gradient = jnp.concatenate([a[cut:] for a in halves], axis=0)
    return dq, dk, dv, down_gradient, up_gradient


def solution(mesh):
    tokens = P(("dp", "seq"), None)
    in_specs = (tokens,) * 5 + (P(), P(), P("dp", None), P("dp", None))
    out_specs = (tokens,) * 3 + (P("dp", None), P(None, "dp"))
    return jax.shard_map(
        per_device, mesh=mesh, in_specs=in_specs, out_specs=out_specs, check_vma=False
    )
```

```python
import functools
import math

import jax
import jax.numpy as jnp
from jax import lax
from jax.experimental import pallas as pl
from jax.experimental.pallas import tpu as pltpu
from jax.sharding import PartitionSpec as P

HEAD_DIM = 128
VERSIONS = 4

adapter_scale = 0.5
masked_score = -1e30
VMEM_LIMIT = 60 * 1024 * 1024
HEADS_PER_STEP = 4


def contract(a, b, dim_a, dim_b):
    return lax.dot_general(
        a, b, (((dim_a,), (dim_b,)), ((), ())), preferred_element_type=jnp.float32
    )


def shifted(block, axis, target):
    count = lax.axis_size(axis)
    route = [(i, target(i) % count) for i in range(count)]
    return lax.ppermute(block, axis, route)


def prepare_kernel(
    place, x, down, up, frozen, keys, queries, grads,
    pair_out, ring_out, query_out, value_out, x_out,
    x_in, down_in, up_in, frozen_in, moved, values_v, low_v, sems,
):
    rows, rank = low_v.shape
    half = values_v.shape[2]
    y = place[0]
    own = pl.multiple_of(y * half, half)
    other = pl.multiple_of((1 - y) * half, half)
    used = []

    def copy(src, dst):
        done = pltpu.make_async_copy(src, dst, sems.at[len(used)])
        used.append(done)
        done.start()
        return done

    chunks = 4
    size = x.shape[1] // chunks
    parts = []
    for c in range(chunks):
        span = pl.ds(c * size, size)
        parts.append((copy(x.at[:, span], x_in.at[:, span]), copy(down.at[span], down_in.at[span])))
    left, right = pl.ds(0, half), pl.ds(half, half)
    route = [
        (keys, other, pair_out.at[:, left]),
        (keys, own, ring_out.at[:, left]),
        (queries, other, query_out.at[:, left]),
        (grads, other, query_out.at[:, right]),
    ]
    arriving = [copy(src.at[:, pl.ds(at, half)], moved.at[i]) for i, (src, at, _) in enumerate(route)]
    up_done = copy(up, up_in)
    frozen_done = copy(frozen, frozen_in)
    low = jnp.zeros((rows, rank), jnp.float32)
    for c, (a, b) in enumerate(parts):
        a.wait()
        b.wait()
        low += contract(x_in[:, c * size : (c + 1) * size], down_in[c * size : (c + 1) * size, :], 1, 0)
    low = low.astype(jnp.bfloat16)
    low_v[...] = low
    rest = []
    members = x_out.shape[0]
    share = x.shape[1] // (2 * members)
    for p in range(members):
        for slot in range(2):
            first = (4 * (p // 2) + 2 * slot + p % 2) * share
            rest.append(copy(x_in.at[:, pl.ds(first, share)], x_out.at[p, :, pl.ds(slot * share, share)]))
    for target in (pair_out.at[:, pl.ds(half, rank)], ring_out.at[:, pl.ds(2 * half, rank)]):
        rest.append(copy(low_v, target))
    for i, done in enumerate(arriving):
        done.wait()
        rest.append(copy(moved.at[i], route[i][2]))
    up_done.wait()
    frozen_done.wait()
    for i, (start, target) in enumerate(((own, ring_out.at[:, right]), (other, value_out))):
        lifted = contract(low, up_in[:, pl.ds(start, half)], 1, 0)
        base = frozen_in[:, pl.ds(start, half)].astype(jnp.float32)
        values_v[i] = (base + adapter_scale * lifted).astype(jnp.bfloat16)
        rest.append(copy(values_v.at[i], target))
    for done in rest:
        done.wait()


def prepare(place, x, down, up, frozen, keys, queries, grads, members):
    rows, width = keys.shape
    rank = down.shape[1]
    half = width // 2
    kind = jnp.bfloat16
    shapes = [
        (rows, half + rank), (rows, width + rank), (rows, width), (rows, half),
        (members, rows, x.shape[1] // members),
    ]
    anywhere = pl.BlockSpec(memory_space=pl.ANY)
    return pl.pallas_call(
        prepare_kernel,
        out_shape=[jax.ShapeDtypeStruct(s, kind) for s in shapes],
        in_specs=[pl.BlockSpec(memory_space=pltpu.SMEM)] + [anywhere] * 7,
        out_specs=[anywhere] * 5,
        scratch_shapes=[
            pltpu.VMEM(x.shape, kind),
            pltpu.VMEM(down.shape, kind),
            pltpu.VMEM(up.shape, kind),
            pltpu.VMEM(frozen.shape, kind),
            pltpu.VMEM((4, rows, half), kind),
            pltpu.VMEM((2, rows, half), kind),
            pltpu.VMEM((rows, rank), kind),
            pltpu.SemaphoreType.DMA((22 + 2 * members,)),
        ],
        compiler_params=pltpu.CompilerParams(vmem_limit_bytes=VMEM_LIMIT),
    )(place, x, down, up, frozen, keys, queries, grads)


def gather(refs, cols):
    return jnp.concatenate([r[:, cols] for r in refs], axis=0)


def against(main, far_a, far_b, other):
    rows = far_a.shape[0]
    far = jnp.concatenate(
        [contract(far_a, other[:rows], 1, 1), contract(far_b, other[rows:], 1, 1)], axis=1
    )
    return jnp.concatenate([contract(main, other, 1, 1), far], axis=0)


def onto(grid, other):
    rows = other.shape[0] // 2
    near = 4 * rows
    return (
        contract(grid[:near], other, 1, 0),
        contract(grid[near:, :rows], other[:rows], 1, 0),
        contract(grid[near:, rows:], other[rows:], 1, 0),
    )


def ordered(order, own, pair, prev, prev2, nxt, nxt2):
    pick = lambda a, b: (a, b) if order == 0 else (b, a)
    mid0, mid1 = pick(own, pair)
    far_prev, near_prev = pick(prev, prev2)
    near_next, far_next = pick(nxt, nxt2)
    return (near_prev, mid0, mid1, near_next), far_prev, far_next


def scatter(order, mid, prev, nxt, cols, main, far_a, far_b):
    rows = far_a.shape[0]
    first, second = (0, rows) if order == 0 else (rows, 0)

    def put(ref, at, val):
        ref[at : at + rows, cols] = val

    put(prev, second, main[:rows])
    put(mid, first, main[rows : 2 * rows])
    put(mid, second, main[2 * rows : 3 * rows])
    put(nxt, first, main[3 * rows :])
    put(prev, first, far_a)
    put(nxt, second, far_b)


def forward_kernel(
    place, lengths, versions,
    q_own, q_pair, g_own, g_pair,
    k_own, k_pair, k_prev, k_prev2, k_next, k_next2,
    l_own, l_pair, l_prev, l_prev2, l_next, l_next2,
    up,
    mid, prev, nxt, back_mid, back_prev, back_next, up_send, probs, scaled,
    bias, weight, dvs,
):
    rows = q_own.shape[0]
    documents = lengths.shape[1]
    step = pl.program_id(0)
    y, z = place[0], place[1]
    base = 2 * z * rows
    heads = dvs.shape[1] // HEAD_DIM

    @pl.when(step == 0)
    def _():
        ends, total = [], jnp.int32(0)
        for j in range(documents):
            total = total + lengths[0, j]
            ends.append(total)
        for b in range(2):
            pos = lax.broadcasted_iota(jnp.int32, (8, rows), 1) + base + b * rows
            first = jnp.zeros_like(pos)
            last = jnp.zeros_like(pos)
            for j in range(documents):
                first = jnp.where(pos >= ends[j], ends[j], first)
            for j in reversed(range(documents)):
                last = jnp.where(pos < ends[j], ends[j], last)
            first, last = first[:1], last[:1]
            for c, shift in enumerate((-1, 0, 1, 2, -2 if b == 0 else 3)):
                key_pos = lax.broadcasted_iota(jnp.int32, (rows, rows), 0) + base + shift * rows
                inside = (key_pos >= first) & (key_pos < last)
                bias[c * rows : (c + 1) * rows, b * rows : (b + 1) * rows] = jnp.where(
                    inside, jnp.float32(0.0), jnp.float32(masked_score)
                )
            row_pos = lax.broadcasted_iota(jnp.int32, (rows, HEAD_DIM), 0) + base + b * rows
            scale = jnp.zeros((rows, HEAD_DIM), jnp.float32)
            for j in range(documents):
                level = lax.shift_left(jnp.int32(1), versions[0, j]).astype(jnp.float32)
                level = level * (2.0 ** (1 - VERSIONS))
                begin = ends[j - 1] if j > 0 else 0
                scale = jnp.where(row_pos >= begin, level, scale)
            weight[b * rows : (b + 1) * rows, :] = scale

    factor = math.log2(math.e) / math.sqrt(HEAD_DIM)
    near = 4 * rows

    def work(order):
        pick = lambda own, pair: (own, pair) if order == 0 else (pair, own)
        ks, k_fp, k_fn = ordered(order, k_own, k_pair, k_prev, k_prev2, k_next, k_next2)
        for h in range(HEADS_PER_STEP):
            cols = slice(h * HEAD_DIM, (h + 1) * HEAD_DIM)
            q = gather(pick(q_own, q_pair), cols)
            g = weight[...] * gather(pick(g_own, g_pair), cols).astype(jnp.float32)
            g = g.astype(jnp.bfloat16)
            scaled[:, cols] = g
            s = against(gather(ks, cols), k_fp[:, cols], k_fn[:, cols], q) * factor + bias[...]
            e = jnp.exp2(s - jnp.max(s, axis=0, keepdims=True))
            p = (e * (1.0 / jnp.sum(e, axis=0, keepdims=True))).astype(jnp.bfloat16)
            probs[h] = p
            small = [a.astype(jnp.bfloat16) for a in onto(p, g)]
            scatter(order, mid, prev, nxt, cols, *small)
            at = step * (HEADS_PER_STEP * HEAD_DIM)
            at = pl.ds(pl.multiple_of(at, HEAD_DIM) + h * HEAD_DIM, HEAD_DIM)
            dvs[:near, at] = small[0]
            dvs[near : near + rows, at] = small[1]
            dvs[near + rows :, at] = small[2]

        @pl.when(step == pl.num_programs(0) - 1)
        def _():
            ls, l_fp, l_fn = ordered(order, l_own, l_pair, l_prev, l_prev2, l_next, l_next2)
            low = jnp.concatenate([r[...] for r in (*ls, l_fp, l_fn)], axis=0)
            part = contract(low, dvs[...], 0, 0).astype(jnp.bfloat16)
            for h in range(2 * heads):
                slot = slice((1 + (h // 2) % 2) * HEAD_DIM, (2 + (h // 2) % 2) * HEAD_DIM)
                local = h - order * heads
                if 0 <= local < heads:
                    block = part[:, local * HEAD_DIM : (local + 1) * HEAD_DIM]
                else:
                    block = jnp.zeros((part.shape[0], HEAD_DIM), jnp.bfloat16)
                up_send[2 * (h // 4) + h % 2, :, slot] = block
            up_send[:, :, :HEAD_DIM] = jnp.zeros(up_send.shape[:2] + (HEAD_DIM,), jnp.bfloat16)
            full = contract(dvs[...], up[...], 1, 1)
            a, b = (0, rows) if order == 0 else (rows, 0)
            places = (
                (back_prev, b), (back_mid, a), (back_mid, b), (back_next, a), (back_prev, a), (back_next, b),
            )
            for c, (ref, at) in enumerate(places):
                ref[at : at + rows, :] = full[c * rows : (c + 1) * rows]

    for order in range(2):
        pl.when(y == order)(functools.partial(work, order))


def backward_kernel(
    place,
    q_own, q_pair, scaled, probs,
    k_own, k_pair, k_prev, k_prev2, k_next, k_next2,
    v_own, v_pair, v_prev, v_prev2, v_next, v_next2,
    dq_own, dq_pair, mid, prev, nxt,
):
    rows = q_own.shape[0]
    near = 4 * rows
    score_scale = 1.0 / math.sqrt(HEAD_DIM)

    def work(order):
        pick = lambda own, pair: (own, pair) if order == 0 else (pair, own)
        ks, k_fp, k_fn = ordered(order, k_own, k_pair, k_prev, k_prev2, k_next, k_next2)
        vs, v_fp, v_fn = ordered(order, v_own, v_pair, v_prev, v_prev2, v_next, v_next2)
        dq0, dq1 = pick(dq_own, dq_pair)
        for h in range(HEADS_PER_STEP):
            cols = slice(h * HEAD_DIM, (h + 1) * HEAD_DIM)
            q = gather(pick(q_own, q_pair), cols)
            dp = against(gather(vs, cols), v_fp[:, cols], v_fn[:, cols], scaled[:, cols])
            wide = probs[h].astype(jnp.float32)
            delta = jnp.sum(wide * dp, axis=0, keepdims=True)
            ds = (wide * (dp - delta)).astype(jnp.bfloat16)
            small = [(score_scale * a).astype(jnp.bfloat16) for a in onto(ds, q)]
            scatter(order, mid, prev, nxt, cols, *small)
            far = jnp.concatenate(
                [
                    contract(ds[near:, :rows], k_fp[:, cols], 0, 0),
                    contract(ds[near:, rows:], k_fn[:, cols], 0, 0),
                ],
                axis=0,
            )
            dq = contract(ds[:near], gather(ks, cols), 0, 0) + far
            dq = (dq * score_scale).astype(jnp.bfloat16)
            dq0[:, cols] = dq[:rows]
            dq1[:, cols] = dq[rows:]

    for order in range(2):
        pl.when(place[0] == order)(functools.partial(work, order))


def forward(place, lengths, versions, queries, grads, keys, ring, up, pair_q, pair, prev, prev2, nxt, nxt2):
    rows, width = queries.shape
    rank = up.shape[0]
    half = width // 2
    heads = half // HEAD_DIM
    block = HEADS_PER_STEP * HEAD_DIM
    steps = heads // HEADS_PER_STEP
    at = lambda first: pl.BlockSpec((rows, block), lambda h, *_: (0, first + h))
    mine = pl.BlockSpec((rows, block), lambda h, pc, *_: (0, pc[0] * steps + h))
    low_at = lambda b: pl.BlockSpec((rows, rank), lambda h, *_: (0, b))
    kind = jnp.bfloat16
    last = half // rank
    in_specs = [
        mine, at(0), mine, at(steps),
        mine, at(0), at(0), at(0), at(0), at(0),
        low_at(2 * last), low_at(last), low_at(2 * last), low_at(last), low_at(2 * last), low_at(last),
        pl.BlockSpec((rank, half), lambda h, pc, *_: (0, pc[0])),
    ]
    operands = (
        queries, pair_q, grads, pair_q,
        keys, pair, prev, prev2, nxt, nxt2,
        ring, pair, prev, prev2, nxt, nxt2,
        up,
    )
    double = jax.ShapeDtypeStruct((2 * rows, half), kind)
    back = jax.ShapeDtypeStruct((2 * rows, rank), jnp.float32)
    double_spec = pl.BlockSpec((2 * rows, block), lambda h, *_: (0, h))
    back_spec = pl.BlockSpec((2 * rows, rank), lambda h, *_: (0, 0))
    out_shape = [
        double, double, double,
        back, back, back,
        jax.ShapeDtypeStruct((heads, rank, 3 * HEAD_DIM), kind),
        jax.ShapeDtypeStruct((heads, 5 * rows, 2 * rows), kind),
        double,
    ]
    out_specs = [
        double_spec, double_spec, double_spec,
        back_spec, back_spec, back_spec,
        pl.BlockSpec((heads, rank, 3 * HEAD_DIM), lambda h, *_: (0, 0, 0)),
        pl.BlockSpec((HEADS_PER_STEP, 5 * rows, 2 * rows), lambda h, *_: (h, 0, 0)),
        double_spec,
    ]
    pairs = 10 * rows * rows * heads
    return pl.pallas_call(
        forward_kernel,
        grid_spec=pltpu.PrefetchScalarGridSpec(
            num_scalar_prefetch=3,
            grid=(steps,),
            in_specs=in_specs,
            out_specs=out_specs,
            scratch_shapes=[
                pltpu.VMEM((5 * rows, 2 * rows), jnp.float32),
                pltpu.VMEM((2 * rows, HEAD_DIM), jnp.float32),
                pltpu.VMEM((6 * rows, half), kind),
            ],
        ),
        out_shape=out_shape,
        compiler_params=pltpu.CompilerParams(
            vmem_limit_bytes=VMEM_LIMIT, dimension_semantics=("arbitrary",)
        ),
        cost_estimate=pl.CostEstimate(
            flops=10 * pairs * HEAD_DIM, bytes_accessed=12 << 20, transcendentals=pairs
        ),
    )(place, lengths, versions, *operands)


def backward(place, queries, keys, scaled, probs, pair_q, k_pair, k_prev2, k_next2, ring, v_pair, prev, v_prev2, nxt, v_next2):
    rows, width = queries.shape
    half = width // 2
    heads = half // HEAD_DIM
    block = HEADS_PER_STEP * HEAD_DIM
    steps = heads // HEADS_PER_STEP
    at = pl.BlockSpec((rows, block), lambda h, *_: (0, h))
    high = pl.BlockSpec((rows, block), lambda h, *_: (0, steps + h))
    mine = pl.BlockSpec((rows, block), lambda h, pc, *_: (0, pc[0] * steps + h))
    kind = jnp.bfloat16
    double = jax.ShapeDtypeStruct((2 * rows, half), kind)
    double_spec = pl.BlockSpec((2 * rows, block), lambda h, *_: (0, h))
    in_specs = [
        mine, at, double_spec,
        pl.BlockSpec((HEADS_PER_STEP, 5 * rows, 2 * rows), lambda h, *_: (h, 0, 0)),
        mine,
    ] + [at] * 5 + [high, at, high, at, high, at]
    single = jax.ShapeDtypeStruct((rows, half), kind)
    pairs = 10 * rows * rows * heads
    return pl.pallas_call(
        backward_kernel,
        grid_spec=pltpu.PrefetchScalarGridSpec(
            num_scalar_prefetch=1,
            grid=(steps,),
            in_specs=in_specs,
            out_specs=[at, at, double_spec, double_spec, double_spec],
        ),
        out_shape=[single, single, double, double, double],
        compiler_params=pltpu.CompilerParams(
            vmem_limit_bytes=VMEM_LIMIT, dimension_semantics=("arbitrary",)
        ),
        cost_estimate=pl.CostEstimate(
            flops=10 * pairs * HEAD_DIM, bytes_accessed=12 << 20, transcendentals=0
        ),
    )(
        place, queries, pair_q, scaled, probs,
        keys, k_pair, prev, k_prev2, nxt, k_next2, ring, v_pair, prev, v_prev2, nxt, v_next2,
    )


def finish_kernel(place, x_cols, both, own, to_low, to_high, to_both, *, norm):
    members, rows, width = x_cols.shape
    rank = both.shape[1]
    x = x_cols[...].reshape(members * rows, width)
    back_rows = both[:, :, :rank].reshape(members * rows, rank)
    down = contract(x, back_rows, 0, 0) * norm
    up = both[0, :, rank:].astype(jnp.float32)
    for i in range(1, members):
        up = up + both[i, :, rank:].astype(jnp.float32)
    up = up * norm
    cut, half = width // 4, rank // 2
    low, high = place[0], place[2]

    def write(a, b):
        refs = (own, to_low, to_high, to_both)
        for slot in range(2):
            for part in range(2):
                ref = refs[2 * (slot ^ b) + (part ^ a)]
                first = (2 * slot + part) * cut
                ref[:cut] = down[first : first + cut]
                ref[cut:] = up[part * half : (part + 1) * half, slot * HEAD_DIM : (slot + 1) * HEAD_DIM]

    for a in range(2):
        for b in range(2):
            pl.when((low == a) & (high == b))(functools.partial(write, a, b))


def simple(kernel, out_shape, place, *operands):
    smem, spec = pl.BlockSpec(memory_space=pltpu.SMEM), pl.BlockSpec(memory_space=pltpu.VMEM)
    return pl.pallas_call(
        kernel,
        out_shape=out_shape,
        in_specs=[smem] + [spec] * len(operands),
        out_specs=[spec] * len(out_shape),
        compiler_params=pltpu.CompilerParams(vmem_limit_bytes=VMEM_LIMIT),
    )(place, *operands)


def per_device(
    normed_input, queries, rotated_key_rows, frozen_value_rows, cotangent,
    adapter_down_weight, adapter_up_weight, document_lengths, versions,
):
    rows, width = queries.shape
    half = width // 2
    rank = adapter_down_weight.shape[1]
    sequence_count = lax.axis_size("seq")
    replicas = lax.axis_size("dp")
    shard = lax.axis_index("seq")
    y, z, high = shard % 2, shard // 2, (lax.axis_index("dp") // 2) % 2
    place = jnp.stack([y, z, high]).astype(jnp.int32)
    to_pair = lambda a: shifted(a, "seq", lambda i: i ^ 1)
    to_next = lambda a: shifted(a, "seq", lambda i: i + 2)
    to_prev = lambda a: shifted(a, "seq", lambda i: i - 2)
    to_high = lambda a: shifted(a, "dp", lambda i: i ^ 2)
    crossed = [
        (i * sequence_count + j, (i ^ 2) * sequence_count + (j ^ 1))
        for i in range(replicas) for j in range(sequence_count)
    ]
    to_both = lambda a: lax.ppermute(a, ("dp", "seq"), crossed)
    after = lambda *a: lax.optimization_barrier(a)
    shape = jax.ShapeDtypeStruct
    wide, narrow = jnp.float32, jnp.bfloat16
    members = replicas // 2
    flat = [[i for i in range(replicas) if (i // 2) % 2 == b] for b in range(2)]

    k_send, ring, q_send, v_send, x_send = prepare(
        place, normed_input, adapter_down_weight, adapter_up_weight, frozen_value_rows,
        rotated_key_rows, queries, cotangent, members,
    )
    k_pair, prev, nxt = to_pair(k_send), to_next(ring), to_prev(ring)
    k_pair, q_send, v_send = after(k_pair, q_send, v_send)
    k_prev2, k_next2 = to_next(k_pair), to_prev(k_pair)
    q_pair, v_pair = to_pair(q_send), to_pair(v_send)
    x_cols = lax.all_to_all(x_send, "dp", 0, 0, tiled=True, axis_index_groups=flat)
    q_pair, v_pair = after(q_pair, v_pair)

    dv_mid, dv_prev, dv_next, back, back_prev, back_next, up_send, probs, scaled = forward(
        place, document_lengths, versions, queries, cotangent, rotated_key_rows, ring,
        adapter_up_weight, q_pair, k_pair, prev, k_prev2, nxt, k_next2,
    )
    from_next, from_prev = to_prev(back_prev), to_next(back_next)
    v_prev2, v_next2 = to_next(v_pair), to_prev(v_pair)
    theirs = to_pair(back[rows:] + from_next[rows:] + from_prev[rows:])
    theirs, v_prev2, v_next2, x_cols = after(theirs, v_prev2, v_next2, x_cols)
    back_rows = (back[:rows] + from_next[:rows] + from_prev[:rows] + theirs).astype(narrow)
    payload = up_send.at[:, :, :rank].set(jnp.broadcast_to(back_rows[None], (members, rows, rank)))
    parts = lax.all_to_all(payload, "dp", 0, 0, tiled=True, axis_index_groups=flat)

    add = lambda a, b, c: (a.astype(wide) + b.astype(wide) + c.astype(wide)).astype(narrow)
    dv = add(dv_mid, to_prev(dv_prev), to_next(dv_next))
    scaled, dv = after(scaled, dv)
    dv_came = to_pair(dv[rows:])
    dq_own, dq_pair, dk_mid, dk_prev, dk_next = backward(
        place, queries, rotated_key_rows, scaled, probs, q_pair, k_pair, k_prev2, k_next2,
        ring, v_pair, prev, v_prev2, nxt, v_next2,
    )
    dk = add(dk_mid, to_prev(dk_prev), to_next(dk_next))

    norm = adapter_scale / math.sqrt(rows * sequence_count * replicas)
    down_rows = adapter_down_weight.shape[0] // replicas
    piece = shape(((down_rows + rank) // 2, rank), wide)
    parts, dk_prev, dk_next, dv_came = after(parts, dk_prev, dk_next, dv_came)
    keep, a, b, c = simple(functools.partial(finish_kernel, norm=norm), [piece] * 4, place, x_cols, parts)
    a, b, c = to_pair(a), to_high(b), to_both(c)
    dq_came, dk_came = to_pair(dq_pair), to_pair(dk[rows:])
    keep = (keep + a + b + c).astype(narrow)
    count = sequence_count // 2
    columns = [list(range(c, sequence_count, 2)) for c in range(2)]
    sums = lax.all_to_all(
        jnp.broadcast_to(keep[None], (count,) + keep.shape), "seq", 0, 0, tiled=True, axis_index_groups=columns
    )
    def joined(a, b):
        return jnp.concatenate([jnp.where(y == 0, a, b), jnp.where(y == 0, b, a)], axis=1)

    dk, dv, dq = joined(dk[:rows], dk_came), joined(dv[:rows], dv_came), joined(dq_own, dq_came)
    sums, dv, dq = after(sums, dv, dq)
    mine = jnp.sum(sums.astype(wide), axis=0)
    other = to_pair(mine)
    halves = [jnp.where(y == 0, mine, other), jnp.where(y == 0, other, mine)]
    cut = down_rows // 2
    down_gradient = jnp.concatenate([a[:cut] for a in halves], axis=0)
    up_gradient = jnp.concatenate([a[cut:] for a in halves], axis=0)
    return dq, dk, dv, down_gradient, up_gradient


def solution(mesh):
    tokens = P(("dp", "seq"), None)
    in_specs = (tokens,) * 5 + (P(), P(), P("dp", None), P("dp", None))
    out_specs = (tokens,) * 3 + (P("dp", None), P(None, "dp"))
    return jax.shard_map(
        per_device, mesh=mesh, in_specs=in_specs, out_specs=out_specs, check_vma=False
    )
```

```python
import functools
import math

import jax
import jax.numpy as jnp
from jax import lax
from jax.experimental import pallas as pl
from jax.experimental.pallas import tpu as pltpu
from jax.sharding import PartitionSpec as P

HEAD_DIM = 128
VERSIONS = 4

adapter_scale = 0.5
masked_score = -1e30
VMEM_LIMIT = 60 * 1024 * 1024
HEADS_PER_STEP = 4


def contract(a, b, dim_a, dim_b):
    return lax.dot_general(
        a, b, (((dim_a,), (dim_b,)), ((), ())), preferred_element_type=jnp.float32
    )


def shifted(block, axis, target):
    count = lax.axis_size(axis)
    route = [(i, target(i) % count) for i in range(count)]
    return lax.ppermute(block, axis, route)


def prepare_kernel(
    place, x, down, up, frozen, keys, queries, grads,
    pair_out, ring_out, query_out, value_out, x_out,
    x_in, down_in, up_in, frozen_in, moved, values_v, low_v, sems,
):
    rows, rank = low_v.shape
    half = values_v.shape[2]
    y = place[0]
    own = pl.multiple_of(y * half, half)
    other = pl.multiple_of((1 - y) * half, half)
    used = []

    def copy(src, dst):
        done = pltpu.make_async_copy(src, dst, sems.at[len(used)])
        used.append(done)
        done.start()
        return done

    chunks = 4
    size = x.shape[1] // chunks
    parts = []
    for c in range(chunks):
        span = pl.ds(c * size, size)
        parts.append((copy(x.at[:, span], x_in.at[:, span]), copy(down.at[span], down_in.at[span])))
    left, right = pl.ds(0, half), pl.ds(half, half)
    route = [
        (keys, other, pair_out.at[:, left]),
        (keys, own, ring_out.at[:, left]),
        (queries, other, query_out.at[:, left]),
        (grads, other, query_out.at[:, right]),
    ]
    arriving = [copy(src.at[:, pl.ds(at, half)], moved.at[i]) for i, (src, at, _) in enumerate(route)]
    up_done = copy(up, up_in)
    frozen_done = copy(frozen, frozen_in)
    low = jnp.zeros((rows, rank), jnp.float32)
    for c, (a, b) in enumerate(parts):
        a.wait()
        b.wait()
        low += contract(x_in[:, c * size : (c + 1) * size], down_in[c * size : (c + 1) * size, :], 1, 0)
    low = low.astype(jnp.bfloat16)
    low_v[...] = low
    rest = []
    members = x_out.shape[0]
    share = x.shape[1] // (2 * members)
    for p in range(members):
        for slot in range(2):
            first = (4 * (p // 2) + 2 * slot + p % 2) * share
            rest.append(copy(x_in.at[:, pl.ds(first, share)], x_out.at[p, :, pl.ds(slot * share, share)]))
    for target in (pair_out.at[:, pl.ds(half, rank)], ring_out.at[:, pl.ds(2 * half, rank)]):
        rest.append(copy(low_v, target))
    for i, done in enumerate(arriving):
        done.wait()
        rest.append(copy(moved.at[i], route[i][2]))
    up_done.wait()
    frozen_done.wait()
    for i, (start, target) in enumerate(((own, ring_out.at[:, right]), (other, value_out))):
        lifted = contract(low, up_in[:, pl.ds(start, half)], 1, 0)
        base = frozen_in[:, pl.ds(start, half)].astype(jnp.float32)
        values_v[i] = (base + adapter_scale * lifted).astype(jnp.bfloat16)
        rest.append(copy(values_v.at[i], target))
    for done in rest:
        done.wait()


def prepare(place, x, down, up, frozen, keys, queries, grads, members):
    rows, width = keys.shape
    rank = down.shape[1]
    half = width // 2
    kind = jnp.bfloat16
    shapes = [
        (rows, half + rank), (rows, width + rank), (rows, width), (rows, half),
        (members, rows, x.shape[1] // members),
    ]
    anywhere = pl.BlockSpec(memory_space=pl.ANY)
    return pl.pallas_call(
        prepare_kernel,
        out_shape=[jax.ShapeDtypeStruct(s, kind) for s in shapes],
        in_specs=[pl.BlockSpec(memory_space=pltpu.SMEM)] + [anywhere] * 7,
        out_specs=[anywhere] * 5,
        scratch_shapes=[
            pltpu.VMEM(x.shape, kind),
            pltpu.VMEM(down.shape, kind),
            pltpu.VMEM(up.shape, kind),
            pltpu.VMEM(frozen.shape, kind),
            pltpu.VMEM((4, rows, half), kind),
            pltpu.VMEM((2, rows, half), kind),
            pltpu.VMEM((rows, rank), kind),
            pltpu.SemaphoreType.DMA((22 + 2 * members,)),
        ],
        compiler_params=pltpu.CompilerParams(vmem_limit_bytes=VMEM_LIMIT),
    )(place, x, down, up, frozen, keys, queries, grads)


def gather(refs, cols):
    return jnp.concatenate([r[:, cols] for r in refs], axis=0)


def against(main, far_a, far_b, other):
    rows = far_a.shape[0]
    far = jnp.concatenate(
        [contract(far_a, other[:rows], 1, 1), contract(far_b, other[rows:], 1, 1)], axis=1
    )
    return jnp.concatenate([contract(main, other, 1, 1), far], axis=0)


def onto(grid, other):
    rows = other.shape[0] // 2
    near = 4 * rows
    return (
        contract(grid[:near], other, 1, 0),
        contract(grid[near:, :rows], other[:rows], 1, 0),
        contract(grid[near:, rows:], other[rows:], 1, 0),
    )


def ordered(order, own, pair, prev, prev2, nxt, nxt2):
    pick = lambda a, b: (a, b) if order == 0 else (b, a)
    mid0, mid1 = pick(own, pair)
    far_prev, near_prev = pick(prev, prev2)
    near_next, far_next = pick(nxt, nxt2)
    return (near_prev, mid0, mid1, near_next), far_prev, far_next


def scatter(order, mid, prev, nxt, cols, main, far_a, far_b):
    rows = far_a.shape[0]
    first, second = (0, rows) if order == 0 else (rows, 0)

    def put(ref, at, val):
        ref[at : at + rows, cols] = val

    put(prev, second, main[:rows])
    put(mid, first, main[rows : 2 * rows])
    put(mid, second, main[2 * rows : 3 * rows])
    put(nxt, first, main[3 * rows :])
    put(prev, first, far_a)
    put(nxt, second, far_b)


def forward_kernel(
    place, lengths, versions,
    q_own, q_pair, g_own, g_pair,
    k_own, k_pair, k_prev, k_prev2, k_next, k_next2,
    l_own, l_pair, l_prev, l_prev2, l_next, l_next2,
    up,
    mid, prev, nxt, back_mid, back_prev, back_next, up_send, probs, scaled,
    bias, weight, dvs,
):
    rows = q_own.shape[0]
    documents = lengths.shape[1]
    step = pl.program_id(0)
    y, z = place[0], place[1]
    base = 2 * z * rows
    heads = dvs.shape[1] // HEAD_DIM

    @pl.when(step == 0)
    def _():
        ends, total = [], jnp.int32(0)
        for j in range(documents):
            total = total + lengths[0, j]
            ends.append(total)
        for b in range(2):
            pos = lax.broadcasted_iota(jnp.int32, (8, rows), 1) + base + b * rows
            first = jnp.zeros_like(pos)
            last = jnp.zeros_like(pos)
            for j in range(documents):
                first = jnp.where(pos >= ends[j], ends[j], first)
            for j in reversed(range(documents)):
                last = jnp.where(pos < ends[j], ends[j], last)
            first, last = first[:1], last[:1]
            for c, shift in enumerate((-1, 0, 1, 2, -2 if b == 0 else 3)):
                key_pos = lax.broadcasted_iota(jnp.int32, (rows, rows), 0) + base + shift * rows
                inside = (key_pos >= first) & (key_pos < last)
                bias[c * rows : (c + 1) * rows, b * rows : (b + 1) * rows] = jnp.where(
                    inside, jnp.float32(0.0), jnp.float32(masked_score)
                )
            row_pos = lax.broadcasted_iota(jnp.int32, (rows, HEAD_DIM), 0) + base + b * rows
            scale = jnp.zeros((rows, HEAD_DIM), jnp.float32)
            for j in range(documents):
                level = lax.shift_left(jnp.int32(1), versions[0, j]).astype(jnp.float32)
                level = level * (2.0 ** (1 - VERSIONS))
                begin = ends[j - 1] if j > 0 else 0
                scale = jnp.where(row_pos >= begin, level, scale)
            weight[b * rows : (b + 1) * rows, :] = scale

    factor = math.log2(math.e) / math.sqrt(HEAD_DIM)
    near = 4 * rows

    def work(order):
        pick = lambda own, pair: (own, pair) if order == 0 else (pair, own)
        ks, k_fp, k_fn = ordered(order, k_own, k_pair, k_prev, k_prev2, k_next, k_next2)
        for h in range(HEADS_PER_STEP):
            cols = slice(h * HEAD_DIM, (h + 1) * HEAD_DIM)
            q = gather(pick(q_own, q_pair), cols)
            g = weight[...] * gather(pick(g_own, g_pair), cols).astype(jnp.float32)
            g = g.astype(jnp.bfloat16)
            scaled[:, cols] = g
            s = against(gather(ks, cols), k_fp[:, cols], k_fn[:, cols], q) * factor + bias[...]
            e = jnp.exp2(s - jnp.max(s, axis=0, keepdims=True))
            p = (e * (1.0 / jnp.sum(e, axis=0, keepdims=True))).astype(jnp.bfloat16)
            probs[h] = p
            small = [a.astype(jnp.bfloat16) for a in onto(p, g)]
            scatter(order, mid, prev, nxt, cols, *small)
            at = step * (HEADS_PER_STEP * HEAD_DIM)
            at = pl.ds(pl.multiple_of(at, HEAD_DIM) + h * HEAD_DIM, HEAD_DIM)
            dvs[:near, at] = small[0]
            dvs[near : near + rows, at] = small[1]
            dvs[near + rows :, at] = small[2]

        @pl.when(step == pl.num_programs(0) - 1)
        def _():
            ls, l_fp, l_fn = ordered(order, l_own, l_pair, l_prev, l_prev2, l_next, l_next2)
            low = jnp.concatenate([r[...] for r in (*ls, l_fp, l_fn)], axis=0)
            part = contract(low, dvs[...], 0, 0).astype(jnp.bfloat16)
            for h in range(2 * heads):
                slot = slice((1 + (h // 2) % 2) * HEAD_DIM, (2 + (h // 2) % 2) * HEAD_DIM)
                local = h - order * heads
                if 0 <= local < heads:
                    block = part[:, local * HEAD_DIM : (local + 1) * HEAD_DIM]
                else:
                    block = jnp.zeros((part.shape[0], HEAD_DIM), jnp.bfloat16)
                up_send[2 * (h // 4) + h % 2, :, slot] = block
            up_send[:, :, :HEAD_DIM] = jnp.zeros(up_send.shape[:2] + (HEAD_DIM,), jnp.bfloat16)
            full = contract(dvs[...], up[...], 1, 1)
            a, b = (0, rows) if order == 0 else (rows, 0)
            places = (
                (back_prev, b), (back_mid, a), (back_mid, b), (back_next, a), (back_prev, a), (back_next, b),
            )
            for c, (ref, at) in enumerate(places):
                ref[at : at + rows, :] = full[c * rows : (c + 1) * rows]

    for order in range(2):
        pl.when(y == order)(functools.partial(work, order))


def backward_kernel(
    place,
    q_own, q_pair, scaled, probs,
    k_own, k_pair, k_prev, k_prev2, k_next, k_next2,
    v_own, v_pair, v_prev, v_prev2, v_next, v_next2,
    dq_own, dq_pair, mid, prev, nxt,
):
    rows = q_own.shape[0]
    near = 4 * rows
    score_scale = 1.0 / math.sqrt(HEAD_DIM)

    def work(order):
        pick = lambda own, pair: (own, pair) if order == 0 else (pair, own)
        ks, k_fp, k_fn = ordered(order, k_own, k_pair, k_prev, k_prev2, k_next, k_next2)
        vs, v_fp, v_fn = ordered(order, v_own, v_pair, v_prev, v_prev2, v_next, v_next2)
        dq0, dq1 = pick(dq_own, dq_pair)
        for h in range(HEADS_PER_STEP):
            cols = slice(h * HEAD_DIM, (h + 1) * HEAD_DIM)
            q = gather(pick(q_own, q_pair), cols)
            dp = against(gather(vs, cols), v_fp[:, cols], v_fn[:, cols], scaled[:, cols])
            wide = probs[h].astype(jnp.float32)
            delta = jnp.sum(wide * dp, axis=0, keepdims=True)
            ds = (wide * (dp - delta)).astype(jnp.bfloat16)
            small = [(score_scale * a).astype(jnp.bfloat16) for a in onto(ds, q)]
            scatter(order, mid, prev, nxt, cols, *small)
            far = jnp.concatenate(
                [
                    contract(ds[near:, :rows], k_fp[:, cols], 0, 0),
                    contract(ds[near:, rows:], k_fn[:, cols], 0, 0),
                ],
                axis=0,
            )
            dq = contract(ds[:near], gather(ks, cols), 0, 0) + far
            dq = (dq * score_scale).astype(jnp.bfloat16)
            dq0[:, cols] = dq[:rows]
            dq1[:, cols] = dq[rows:]

    for order in range(2):
        pl.when(place[0] == order)(functools.partial(work, order))


def forward(place, lengths, versions, queries, grads, keys, ring, up, pair_q, pair, prev, prev2, nxt, nxt2):
    rows, width = queries.shape
    rank = up.shape[0]
    half = width // 2
    heads = half // HEAD_DIM
    block = HEADS_PER_STEP * HEAD_DIM
    steps = heads // HEADS_PER_STEP
    at = lambda first: pl.BlockSpec((rows, block), lambda h, *_: (0, first + h))
    mine = pl.BlockSpec((rows, block), lambda h, pc, *_: (0, pc[0] * steps + h))
    low_at = lambda b: pl.BlockSpec((rows, rank), lambda h, *_: (0, b))
    kind = jnp.bfloat16
    last = half // rank
    in_specs = [
        mine, at(0), mine, at(steps),
        mine, at(0), at(0), at(0), at(0), at(0),
        low_at(2 * last), low_at(last), low_at(2 * last), low_at(last), low_at(2 * last), low_at(last),
        pl.BlockSpec((rank, half), lambda h, pc, *_: (0, pc[0])),
    ]
    operands = (
        queries, pair_q, grads, pair_q,
        keys, pair, prev, prev2, nxt, nxt2,
        ring, pair, prev, prev2, nxt, nxt2,
        up,
    )
    double = jax.ShapeDtypeStruct((2 * rows, half), kind)
    back = jax.ShapeDtypeStruct((2 * rows, rank), jnp.float32)
    double_spec = pl.BlockSpec((2 * rows, block), lambda h, *_: (0, h))
    back_spec = pl.BlockSpec((2 * rows, rank), lambda h, *_: (0, 0))
    out_shape = [
        double, double, double,
        back, back, back,
        jax.ShapeDtypeStruct((heads, rank, 3 * HEAD_DIM), kind),
        jax.ShapeDtypeStruct((heads, 5 * rows, 2 * rows), kind),
        double,
    ]
    out_specs = [
        double_spec, double_spec, double_spec,
        back_spec, back_spec, back_spec,
        pl.BlockSpec((heads, rank, 3 * HEAD_DIM), lambda h, *_: (0, 0, 0)),
        pl.BlockSpec((HEADS_PER_STEP, 5 * rows, 2 * rows), lambda h, *_: (h, 0, 0)),
        double_spec,
    ]
    pairs = 10 * rows * rows * heads
    return pl.pallas_call(
        forward_kernel,
        grid_spec=pltpu.PrefetchScalarGridSpec(
            num_scalar_prefetch=3,
            grid=(steps,),
            in_specs=in_specs,
            out_specs=out_specs,
            scratch_shapes=[
                pltpu.VMEM((5 * rows, 2 * rows), jnp.float32),
                pltpu.VMEM((2 * rows, HEAD_DIM), jnp.float32),
                pltpu.VMEM((6 * rows, half), kind),
            ],
        ),
        out_shape=out_shape,
        compiler_params=pltpu.CompilerParams(
            vmem_limit_bytes=VMEM_LIMIT, dimension_semantics=("arbitrary",)
        ),
        cost_estimate=pl.CostEstimate(
            flops=10 * pairs * HEAD_DIM, bytes_accessed=12 << 20, transcendentals=pairs
        ),
    )(place, lengths, versions, *operands)


def backward(place, queries, keys, scaled, probs, pair_q, k_pair, k_prev2, k_next2, ring, v_pair, prev, v_prev2, nxt, v_next2):
    rows, width = queries.shape
    half = width // 2
    heads = half // HEAD_DIM
    block = HEADS_PER_STEP * HEAD_DIM
    steps = heads // HEADS_PER_STEP
    at = pl.BlockSpec((rows, block), lambda h, *_: (0, h))
    high = pl.BlockSpec((rows, block), lambda h, *_: (0, steps + h))
    mine = pl.BlockSpec((rows, block), lambda h, pc, *_: (0, pc[0] * steps + h))
    kind = jnp.bfloat16
    double = jax.ShapeDtypeStruct((2 * rows, half), kind)
    double_spec = pl.BlockSpec((2 * rows, block), lambda h, *_: (0, h))
    in_specs = [
        mine, at, double_spec,
        pl.BlockSpec((HEADS_PER_STEP, 5 * rows, 2 * rows), lambda h, *_: (h, 0, 0)),
        mine,
    ] + [at] * 5 + [high, at, high, at, high, at]
    single = jax.ShapeDtypeStruct((rows, half), kind)
    pairs = 10 * rows * rows * heads
    return pl.pallas_call(
        backward_kernel,
        grid_spec=pltpu.PrefetchScalarGridSpec(
            num_scalar_prefetch=1,
            grid=(steps,),
            in_specs=in_specs,
            out_specs=[at, at, double_spec, double_spec, double_spec],
        ),
        out_shape=[single, single, double, double, double],
        compiler_params=pltpu.CompilerParams(
            vmem_limit_bytes=VMEM_LIMIT, dimension_semantics=("arbitrary",)
        ),
        cost_estimate=pl.CostEstimate(
            flops=10 * pairs * HEAD_DIM, bytes_accessed=12 << 20, transcendentals=0
        ),
    )(
        place, queries, pair_q, scaled, probs,
        keys, k_pair, prev, k_prev2, nxt, k_next2, ring, v_pair, prev, v_prev2, nxt, v_next2,
    )


def finish_kernel(place, x_cols, both, own, to_low, to_high, to_both, *, norm):
    members, rows, width = x_cols.shape
    rank = both.shape[1]
    x = x_cols[...].reshape(members * rows, width)
    back_rows = both[:, :, :rank].reshape(members * rows, rank)
    down = contract(x, back_rows, 0, 0) * norm
    up = both[0, :, rank:].astype(jnp.float32)
    for i in range(1, members):
        up = up + both[i, :, rank:].astype(jnp.float32)
    up = up * norm
    cut, half = width // 4, rank // 2
    low, high = place[0], place[2]

    def write(a, b):
        refs = (own, to_low, to_high, to_both)
        for slot in range(2):
            for part in range(2):
                ref = refs[2 * (slot ^ b) + (part ^ a)]
                first = (2 * slot + part) * cut
                ref[:cut] = down[first : first + cut]
                ref[cut:] = up[part * half : (part + 1) * half, slot * HEAD_DIM : (slot + 1) * HEAD_DIM]

    for a in range(2):
        for b in range(2):
            pl.when((low == a) & (high == b))(functools.partial(write, a, b))


def simple(kernel, out_shape, place, *operands):
    smem, spec = pl.BlockSpec(memory_space=pltpu.SMEM), pl.BlockSpec(memory_space=pltpu.VMEM)
    return pl.pallas_call(
        kernel,
        out_shape=out_shape,
        in_specs=[smem] + [spec] * len(operands),
        out_specs=[spec] * len(out_shape),
        compiler_params=pltpu.CompilerParams(vmem_limit_bytes=12 * 1024 * 1024),
    )(place, *operands)


def per_device(
    normed_input, queries, rotated_key_rows, frozen_value_rows, cotangent,
    adapter_down_weight, adapter_up_weight, document_lengths, versions,
):
    rows, width = queries.shape
    half = width // 2
    rank = adapter_down_weight.shape[1]
    sequence_count = lax.axis_size("seq")
    replicas = lax.axis_size("dp")
    shard = lax.axis_index("seq")
    y, z, high = shard % 2, shard // 2, (lax.axis_index("dp") // 2) % 2
    place = jnp.stack([y, z, high]).astype(jnp.int32)
    to_pair = lambda a: shifted(a, "seq", lambda i: i ^ 1)
    to_next = lambda a: shifted(a, "seq", lambda i: i + 2)
    to_prev = lambda a: shifted(a, "seq", lambda i: i - 2)
    to_high = lambda a: shifted(a, "dp", lambda i: i ^ 2)
    crossed = [
        (i * sequence_count + j, (i ^ 2) * sequence_count + (j ^ 1))
        for i in range(replicas) for j in range(sequence_count)
    ]
    to_both = lambda a: lax.ppermute(a, ("dp", "seq"), crossed)
    after = lambda *a: lax.optimization_barrier(a)
    shape = jax.ShapeDtypeStruct
    wide, narrow = jnp.float32, jnp.bfloat16
    members = replicas // 2
    flat = [[i for i in range(replicas) if (i // 2) % 2 == b] for b in range(2)]

    k_send, ring, q_send, v_send, x_send = prepare(
        place, normed_input, adapter_down_weight, adapter_up_weight, frozen_value_rows,
        rotated_key_rows, queries, cotangent, members,
    )
    k_pair, prev, nxt = to_pair(k_send), to_next(ring), to_prev(ring)
    k_pair, q_send, v_send = after(k_pair, q_send, v_send)
    k_prev2, k_next2 = to_next(k_pair), to_prev(k_pair)
    q_pair, v_pair = to_pair(q_send), to_pair(v_send)
    x_cols = lax.all_to_all(x_send, "dp", 0, 0, tiled=True, axis_index_groups=flat)

    dv_mid, dv_prev, dv_next, back, back_prev, back_next, up_send, probs, scaled = forward(
        place, document_lengths, versions, queries, cotangent, rotated_key_rows, ring,
        adapter_up_weight, q_pair, k_pair, prev, k_prev2, nxt, k_next2,
    )
    v_pair, back_prev = after(v_pair, back_prev)
    from_next, from_prev = to_prev(back_prev), to_next(back_next)
    v_prev2, v_next2 = to_next(v_pair), to_prev(v_pair)
    theirs = to_pair(back[rows:] + from_next[rows:] + from_prev[rows:])
    theirs, v_prev2, v_next2, x_cols = after(theirs, v_prev2, v_next2, x_cols)
    back_rows = (back[:rows] + from_next[:rows] + from_prev[:rows] + theirs).astype(narrow)
    payload = up_send.at[:, :, :rank].set(jnp.broadcast_to(back_rows[None], (members, rows, rank)))
    parts = lax.all_to_all(payload, "dp", 0, 0, tiled=True, axis_index_groups=flat)

    add = lambda a, b, c: (a.astype(wide) + b.astype(wide) + c.astype(wide)).astype(narrow)
    dv = add(dv_mid, to_prev(dv_prev), to_next(dv_next))
    scaled, dv = after(scaled, dv)
    dv_came = to_pair(dv[rows:])
    dq_own, dq_pair, dk_mid, dk_prev, dk_next = backward(
        place, queries, rotated_key_rows, scaled, probs, q_pair, k_pair, k_prev2, k_next2,
        ring, v_pair, prev, v_prev2, nxt, v_next2,
    )
    dk = add(dk_mid, to_prev(dk_prev), to_next(dk_next))

    norm = adapter_scale / math.sqrt(rows * sequence_count * replicas)
    down_rows = adapter_down_weight.shape[0] // replicas
    piece = shape(((down_rows + rank) // 2, rank), wide)
    parts, dk_prev, dk_next, dv_came = after(parts, dk_prev, dk_next, dv_came)
    keep, a, b, c = simple(functools.partial(finish_kernel, norm=norm), [piece] * 4, place, x_cols, parts)
    a, b, c = to_pair(a), to_high(b), to_both(c)
    dq_came, dk_came = to_pair(dq_pair), to_pair(dk[rows:])
    keep = (keep + a + b + c).astype(narrow)
    count = sequence_count // 2
    columns = [list(range(c, sequence_count, 2)) for c in range(2)]
    sums = lax.all_to_all(
        jnp.broadcast_to(keep[None], (count,) + keep.shape), "seq", 0, 0, tiled=True, axis_index_groups=columns
    )
    def joined(a, b):
        return jnp.concatenate([jnp.where(y == 0, a, b), jnp.where(y == 0, b, a)], axis=1)

    dk, dv, dq = joined(dk[:rows], dk_came), joined(dv[:rows], dv_came), joined(dq_own, dq_came)
    sums, dv, dq = after(sums, dv, dq)
    mine = jnp.sum(sums.astype(wide), axis=0)
    other = to_pair(mine)
    halves = [jnp.where(y == 0, mine, other), jnp.where(y == 0, other, mine)]
    cut = down_rows // 2
    down_gradient = jnp.concatenate([a[:cut] for a in halves], axis=0)
    up_gradient = jnp.concatenate([a[cut:] for a in halves], axis=0)
    return dq, dk, dv, down_gradient, up_gradient


def solution(mesh):
    tokens = P(("dp", "seq"), None)
    in_specs = (tokens,) * 5 + (P(), P(), P("dp", None), P("dp", None))
    out_specs = (tokens,) * 3 + (P("dp", None), P(None, "dp"))
    return jax.shard_map(
        per_device, mesh=mesh, in_specs=in_specs, out_specs=out_specs, check_vma=False
    )
```
